32 devices in a mesh: apa: 16 (over z, x, core), chan: 2 (over y).
Axes of the slice: x: 2, y: 2, z: 4, core: 2. Of those that a mesh axis runs over, the one named last changes fastest.
Arguments:
- frames: bfloat16 [16, 2560, 256], P('apa', 'chan'), may hold values from -6 to 6
- link_to_wire: int32 [16, 2560], P('apa'), may hold values from 0 to 2559, each once within a row
- neighbours: int32 [16, 2], P('apa'), may hold values from -1 to 15, as said below
- kernel: float32 [2, 128, 2816], P(None, 'chan'), may hold values from -6 to 6
- wide_filter: float32 [128], replicated, may hold values from 0.3 to 1
- tight_filter: float32 [128], replicated, may hold values from 0.05 to 0.5
- roi_mask: int32 [16, 160, 4], P('apa', 'chan'), may hold values 0 or 1
Outputs:
- deconvolved: float32 [16, 2560, 256], P('apa', 'chan')
The draws below stay inside these ranges and needn't reach their ends.
Inputs may be any that keep to these rules, and one draw needn't show every extreme that they name: `link_to_wire`: each row names every channel once. `neighbours`: the 16 APAs form one chain along the detector: column 0 names the APA before, column 1 the APA after, -1 at the two ends of the chain; every named APA lies on the same index of apa as the naming APA or on an adjacent one.
All inputs are finite; a program needn't handle non-finite values. No bound on the sum of `roi_mask` on one device may be relied on, other than what follows from the above.
Results may differ from the reference program's by a relative error of at most 0.0023.
Values may be sent and summed in bfloat16 or wider, within the bound.
No kernel may reach another device: no remote copies, remote signals or barrier semaphores. Data moves between devices by JAX's collectives and lax.ppermute only.
A program may use at most 128 MiB of HBM per device.

```python
import math
import jax
import jax.numpy as jnp
from jax import lax

PU = 800
PV = 800
PW = 960
TICKS = 256
HALO_CH = 128
BC = 16
BT = 64
APA_DEV = 1
APAS = 16
CHANNELS = 2560
FREQS = 128
KCH = 2816


def draw_neighbours(key, part):
    blocks = APAS // APA_DEV
    keys = jax.random.split(key, blocks)
    inner = jax.vmap(lambda single: jax.random.permutation(single, APA_DEV))(keys)
    offsets = jnp.arange(blocks, dtype=jnp.int32) * APA_DEV
    order = (inner.astype(jnp.int32) + offsets[:, None]).reshape(-1)
    before = jnp.concatenate([jnp.full((1,), -1, jnp.int32), order[:-1]])
    after = jnp.concatenate([order[1:], jnp.full((1,), -1, jnp.int32)])
    lower = jnp.zeros((APAS,), jnp.int32).at[order].set(before)
    upper = jnp.zeros((APAS,), jnp.int32).at[order].set(after)
    return jnp.stack([lower, upper], axis=1)


def with_ends(result, rng, least, largest):
    longest = result.shape.index(max(result.shape))
    spots = []
    for shift in (0, 1):
        where = [jax.random.randint(jax.random.fold_in(rng, axis), (), 0, length) for axis, length in enumerate(result.shape)]
        where[longest] = (where[longest] + shift) % result.shape[longest]
        spots.append(tuple(where))
    return result.at[spots[0]].set(least).at[spots[1]].set(largest)


def levels(own_key, extent, cuts, least, high):
    def one(position, blocks):
        steps = jax.random.uniform(jax.random.fold_in(jax.random.fold_in(own_key, 6), position), (blocks,), jnp.float32, least / len(cuts), high / len(cuts))
        return jnp.repeat(jnp.exp(steps), extent[position] // blocks).reshape((-1,) + (1,) * (len(extent) - position - 1))

    factor_of = one(*cuts[0])
    for cut in cuts[1:]:
        factor_of = factor_of * one(*cut)
    return factor_of


def scatter_about(own_key, dims, scale, bound, shards=(), kind=jnp.bfloat16):
    entries = jax.random.normal(own_key, dims, jnp.float32) * scale
    if len(shards) > 0:
        entries = levels(own_key, dims, shards, -0.22, 0.18) * entries
    return jnp.clip(entries, min=-bound, max=bound).astype(kind)


def setup_inputs(seed: int = 0) -> dict:
    seeds = jax.random.split(jax.random.key(seed), 8)
    frames = scatter_about(seeds[0], (APAS, CHANNELS, TICKS), 1.0, 6.0, ((0, 16), (1, 2)))
    link_to_wire = jax.vmap(lambda own: jax.random.permutation(own, CHANNELS))(jax.random.split(seeds[1], APAS)).reshape((APAS, CHANNELS)).astype(jnp.int32)
    neighbours = draw_neighbours(jax.random.fold_in(seeds[7], 71), 0)
    kernel = scatter_about(seeds[3], (2, FREQS, KCH), 1.0, 6.0, ((1, 2),), jnp.float32)
    wide_filter = jnp.clip(jnp.exp(jax.random.uniform(seeds[4], (FREQS,), jnp.float32, math.log(0.3), math.log(1.0))), 0.3, 1.0)
    tight_filter = jnp.clip(jnp.exp(jax.random.uniform(seeds[5], (FREQS,), jnp.float32, math.log(0.05), math.log(0.5))), 0.05, 0.5)
    roi_mask = with_ends((jax.random.randint(seeds[6], (APAS, CHANNELS // BC, TICKS // BT), 0, 3) < 1).astype(jnp.int32), jax.random.fold_in(seeds[6], 1), 0, 1)
    return {"frames": frames, "link_to_wire": link_to_wire, "neighbours": neighbours, "kernel": kernel, "wide_filter": wide_filter, "tight_filter": tight_filter, "roi_mask": roi_mask}


two_pi = 2.0 * math.pi
highest = lax.Precision.HIGHEST


def tick_angles(ticks):
    moment = lax.iota(jnp.int32, ticks)
    harmonic = lax.iota(jnp.int32, ticks // 2)
    return ((moment[:, None] * harmonic[None, :]) % ticks).astype(jnp.float32) * (two_pi / ticks)


def forward_table(ticks):
    angles = tick_angles(ticks)
    return jnp.concatenate([jnp.cos(angles), -jnp.sin(angles)], axis=1).astype(jnp.bfloat16)


def inverse_basis(ticks, filter_gain):
    angles = tick_angles(ticks).T
    harmonic = lax.iota(jnp.int32, ticks // 2)
    weights = jnp.where(harmonic == 0, 1.0, 2.0).astype(jnp.float32) / ticks * filter_gain
    return jnp.stack([jnp.cos(angles) * weights[:, None], -jnp.sin(angles) * weights[:, None]])


def deconvolve(plane_field, response_part, keep_lo, keep_hi):
    product = jnp.fft.fft(plane_field, axis=-1) * response_part[None]
    return jnp.fft.ifft(product, axis=-1)[:, :, keep_lo:keep_hi]


def reference(frames, link_to_wire, neighbours, kernel, wide_filter, tight_filter, roi_mask):
    apa_index = jnp.arange(APAS, dtype=jnp.int32)[:, None]
    wired = jnp.zeros_like(frames).at[apa_index, link_to_wire].set(frames)
    spectra = jnp.dot(wired.reshape(-1, TICKS), forward_table(TICKS), preferred_element_type=jnp.float32)
    spectra = spectra.reshape(APAS, CHANNELS, 2, FREQS)
    field = jnp.transpose(spectra[:, :, 0] + 1j * spectra[:, :, 1], (0, 2, 1))
    plane_start = PU + PV
    lower_id = neighbours[:, 0]
    upper_id = neighbours[:, 1]
    lower_band = field[:, :, CHANNELS - HALO_CH:]
    upper_band = field[:, :, plane_start:plane_start + HALO_CH]
    lower_rim = lower_band[jnp.maximum(lower_id, 0)] * (lower_id >= 0)[:, None, None]
    upper_rim = upper_band[jnp.maximum(upper_id, 0)] * (upper_id >= 0)[:, None, None]
    extended = jnp.concatenate([lower_rim, field[:, :, plane_start:], upper_rim], axis=2)
    response = kernel[0] + 1j * kernel[1]
    parts = jnp.concatenate([
        deconvolve(field[:, :, :PU], response[:, :PU], 0, PU),
        deconvolve(field[:, :, PU:plane_start], response[:, PU:plane_start], 0, PV),
        deconvolve(extended, response[:, plane_start:], HALO_CH, HALO_CH + PW)], axis=2)
    stacked = jnp.stack([jnp.real(parts).astype(jnp.float32), jnp.imag(parts).astype(jnp.float32)], axis=1)

    def signal(filter_gain):
        return jnp.einsum("azkc,zkt->act", stacked, inverse_basis(TICKS, filter_gain), precision=highest)

    expanded = jnp.repeat(jnp.repeat(roi_mask, BC, axis=1), BT, axis=2)
    return jnp.where(expanded == 1, signal(wide_filter), signal(tight_filter))
```

```python
import functools
import math

import jax
import jax.numpy as jnp
import ml_dtypes
import numpy as np
from jax import lax
from jax.experimental import pallas as pl
from jax.experimental.pallas import tpu as pltpu
from jax.sharding import PartitionSpec as P

PU = 800
PV = 800
PW = 960
HALO_CH = 128
BC = 16
BT = 64
CHANNELS = 2560

two_pi = 2.0 * math.pi
lane = 128
f32 = jnp.float32
bf16 = jnp.bfloat16
whole = pl.BlockSpec(memory_space=pltpu.VMEM)
scalars = pl.BlockSpec(memory_space=pltpu.SMEM)


def ceil_to(size, step):
    return -(-size // step) * step


class Plane:
    def __init__(self, length, wire, count, keep, kernel_start, row):
        self.length, self.wire, self.count, self.keep = length, wire, count, keep
        self.kernel_start, self.row = kernel_start, row
        self.half = length // 2
        self.rows = ceil_to(self.half + 1, 16)


def make_planes():
    found, row, start = [], 0, 0
    for length, wire, count, keep in (
        (PU, 0, PU, 0),
        (PV, PU, PV, 0),
        (PW + 2 * HALO_CH, PU + PV, PW, HALO_CH),
    ):
        found.append(Plane(length, wire, count, keep, start, row))
        row += found[-1].rows
        start += length
    return found


planes = make_planes()
all_rows = planes[-1].row + planes[-1].rows


def split(values):
    high = values.astype(bf16)
    return high, (values - high.astype(f32)).astype(bf16)


def channel_tables(length, rows):
    index = np.arange(rows)
    angles = (index[:, None] * index[None, :] % length) * (two_pi / length)
    inside = (index <= length // 2).astype(np.float64)
    mask = inside[:, None] * inside[None, :]
    parts = []
    for values in (np.cos(angles) * mask, np.sin(angles) * mask):
        high = values.astype(np.float32).astype(ml_dtypes.bfloat16)
        parts += [high, (values - high.astype(np.float64)).astype(np.float32).astype(ml_dtypes.bfloat16)]
    return np.stack(parts)


def tick_angles(ticks):
    return (np.arange(ticks)[:, None] * np.arange(ticks // 2)[None, :] % ticks) * (two_pi / ticks)


def in_blocks(values, blocks, padded):
    parts = np.stack(np.split(values, blocks, axis=-1))
    return np.pad(parts, [(0, 0)] * (parts.ndim - 1) + [(0, padded - parts.shape[-1])])


def forward_tables(ticks, blocks, padded):
    angles = tick_angles(ticks)
    halves = [in_blocks(part, blocks, padded) for part in (np.cos(angles), -np.sin(angles))]
    return np.concatenate(halves, axis=-1).astype(np.float32).astype(ml_dtypes.bfloat16)


def inverse_tables(ticks, blocks, padded):
    angles = tick_angles(ticks)
    weights = np.where(np.arange(ticks // 2) == 0, 1.0, 2.0) / ticks
    halves = [in_blocks(part * weights, blocks, padded) for part in (np.cos(angles), -np.sin(angles))]
    return np.ascontiguousarray(np.swapaxes(np.concatenate(halves, axis=-1), 1, 2)).astype(np.float32)


def dot(left, right):
    return jnp.dot(left, right, preferred_element_type=f32)


def one_hot(rows, first, targets):
    numbers = lax.broadcasted_iota(jnp.int32, (rows, targets.shape[1]), 0) + first
    return jnp.where(numbers == targets, 1.0, 0.0).astype(bf16)


def far_spectra(blocks, where, frames, table, *outs):
    for shift, out in enumerate(outs, 1):
        out[...] = dot(frames[...], table[lax.rem(where[0] + shift, blocks)]).astype(bf16)


def near_spectra(blocks, where, frames, table, wires, own, *bands):
    spectra = [dot(frames[...], table[lax.rem(where[0] + s, blocks)]).astype(bf16) for s in range(blocks)]
    own[...] = spectra[0]
    for way in range(2):
        chosen = one_hot(HALO_CH, where[1 + way], wires[...])
        for s in range(blocks):
            bands[way * blocks + s][...] = dot(chosen, spectra[s]).astype(bf16)


def rotated(values):
    half = values.shape[1] // 2
    first = lax.broadcasted_iota(jnp.int32, values.shape, 1) < half
    turned = pltpu.roll(values, half, 1)
    return jnp.where(first, turned, -turned)


def fold_operand(spectra, sign_row):
    width = spectra.shape[1]
    signs = jnp.transpose(jnp.broadcast_to(sign_row, (width, sign_row.shape[1])))
    turned = rotated(spectra.astype(f32)) * signs
    return jnp.concatenate([spectra, turned.astype(bf16)], axis=1)


def prepare(share, kernel, targets, signs, own, sums, diffs, folded):
    harmonics, width = kernel.shape[1], sums.shape[1]
    spare = width // 2 - harmonics
    operand = fold_operand(own[...], signs[:, :share])
    for plane in planes:
        rows = pl.ds(plane.row, plane.rows)
        folded[rows, :] = dot(one_hot(plane.rows, plane.row, targets[:, :share]), operand)
        start = plane.kernel_start // lane * lane
        stop = ceil_to(plane.kernel_start + plane.length, lane)
        parts = []
        for z in range(2):
            parts.append(kernel[z, :, start:stop])
            if spare:
                parts.append(jnp.zeros((spare, stop - start), f32))
        high, low = split(jnp.concatenate(parts, axis=0))
        values = jnp.concatenate([high, low], axis=0)
        row = lax.broadcasted_iota(jnp.int32, (plane.rows, stop - start), 0)
        column = lax.broadcasted_iota(jnp.int32, (plane.rows, stop - start), 1) + (start - plane.kernel_start)
        direct = jnp.where((column == row) & (row <= plane.half), 1.0, 0.0)
        mirror = jnp.where((column == plane.length - row) & (row > 0) & (row < plane.half), 1.0, 0.0)
        for out, matrix in ((sums, direct + mirror), (diffs, direct - mirror)):
            both = lax.dot_general(
                matrix.astype(bf16), values, (((1,), (1,)), ((), ())), preferred_element_type=f32
            )
            out[rows, :] = (both[:, :width] + both[:, width:]) * (1.0 / plane.length)


def two_pass(high, low, values):
    width = values.shape[1]
    joined = jnp.concatenate(split(values), axis=1)
    both = dot(high, joined) + dot(low, joined)
    return both[:, :width] + both[:, width:]


def times(values, factor):
    half = values.shape[1] // 2
    first = lax.broadcasted_iota(jnp.int32, values.shape, 1) < half
    other = pltpu.roll(factor, half, 1)
    real = jnp.where(first, factor, other)
    imag = jnp.where(first, other, factor)
    return values * real - rotated(values) * imag


def channel_stage(blocks, share, where, *refs):
    received = refs[: blocks - 1]
    halo = refs[blocks - 1 : 3 * blocks - 1]
    targets, signs, folded, sums, diffs, narrow, wide = refs[3 * blocks - 1 : 3 * blocks + 6]
    own = refs[3 * blocks + 6]
    sends = refs[3 * blocks + 7 : 4 * blocks + 6]
    result = refs[4 * blocks + 6]
    far = (blocks - 1) * share
    spectra = jnp.concatenate([ref[...] for ref in received + halo], axis=0)
    operand = fold_operand(spectra, signs[:, share:])
    for plane in planes:
        rows = pl.ds(plane.row, plane.rows)
        used = operand.shape[0] if plane.keep else far
        wanted = targets[:, share : share + used]
        both = folded[rows, :] + dot(one_hot(plane.rows, plane.row, wanted), operand[:used])
        table = wide if plane.keep else narrow
        width = both.shape[1] // 2
        even = two_pass(table[0], table[1], both[:, :width])
        odd = two_pass(table[2], table[3], both[:, width:])
        plus, minus = sums[rows, :], diffs[rows, :]
        total = times(even, plus) + times(odd, minus)
        gap = times(even, minus) + times(odd, plus)
        kept = slice(plane.keep, plane.rows)
        cosine = two_pass(table[0, kept], table[1, kept], total)
        sine = two_pass(table[2, kept], table[3, kept], -rotated(gap))
        straight = plane.count // 2
        result[plane.wire : plane.wire + straight, :] = (cosine + sine)[:straight]
        back = jnp.concatenate(split(cosine - sine), axis=1)
        row = lax.broadcasted_iota(jnp.int32, (straight, back.shape[0]), 0)
        column = lax.broadcasted_iota(jnp.int32, (straight, back.shape[0]), 1) + plane.keep
        turned = dot(jnp.where(column == plane.half - row, 1.0, 0.0).astype(bf16), back)
        result[plane.wire + straight : plane.wire + plane.count, :] = turned[:, :width] + turned[:, width:]
    here = where[0]
    own[...] = result[pl.ds(pl.multiple_of(here * share, share), share), :]
    for shift, out in enumerate(sends, 1):
        first = pl.multiple_of(lax.rem(here + shift, blocks) * share, share)
        out[...] = result[pl.ds(first, share), :].astype(bf16)


def chosen_signal(both, mask, ticks):
    column = lax.broadcasted_iota(jnp.int32, (mask.shape[0], ticks), 1)
    inside = jnp.zeros((mask.shape[0], ticks), jnp.int32)
    for block in range(ticks // BT):
        inside = jnp.where(column // BT == block, mask[:, block : block + 1], inside)
    inside = jnp.broadcast_to(inside[:, None, :], (mask.shape[0], BC, ticks)).reshape(-1, ticks)
    return jnp.where(inside == 1, both[:, :ticks], both[:, ticks:])


def own_signal(blocks, where, own, basis, mask, signal, bases):
    here = where[0]
    ticks = signal.shape[1]
    high, low = split(basis[here])
    joined = jnp.concatenate(split(own[...]), axis=1)
    both = dot(joined, jnp.concatenate([high, high], axis=0))
    both += dot(joined, jnp.concatenate([low, low], axis=0))
    signal[...] = chosen_signal(both, mask[...], ticks)
    for shift in range(1, blocks):
        parts = split(basis[lax.rem(here + blocks - shift, blocks)])
        bases[shift - 1] = jnp.concatenate(parts, axis=0)


def whole_signal(blocks, signal, bases, mask, *refs):
    out = refs[-1]
    ticks = out.shape[1]
    both = None
    for shift in range(1, blocks):
        values = refs[shift - 1][...]
        term = dot(jnp.concatenate([values, values], axis=1), bases[shift - 1])
        both = term if both is None else both + term
    if both is None:
        out[...] = signal[...]
    else:
        out[...] = signal[...] + chosen_signal(both, mask[...], ticks)


def call(kernel, outs, ins, name, scratch=()):
    return pl.pallas_call(
        kernel,
        out_shape=[jax.ShapeDtypeStruct(shape, dtype) for shape, dtype in outs],
        in_specs=ins,
        out_specs=[whole] * len(outs),
        scratch_shapes=scratch,
        compiler_params=pltpu.CompilerParams(vmem_limit_bytes=48 * 1024 * 1024),
        name=name,
    )


def fold_targets(wires, lower, upper, here, blocks):
    first = wires < PU
    second = wires < PU + PV
    last = planes[2]
    offset = jnp.where(first, wires, jnp.where(second, wires - PU, wires - (PU + PV) + HALO_CH))
    length = jnp.where(first, PU, jnp.where(second, PV, last.length))
    row = jnp.where(first, 0, jnp.where(second, planes[1].row, last.row))
    spot = jnp.tile(lax.iota(jnp.int32, HALO_CH), blocks)
    far = last.length - HALO_CH
    sides = []
    for other in (here - 1, here + 1):
        begin = jnp.where(lower == other, 0, far)
        known = (other >= 0) & ((lower == other) | (upper == other))
        sides.append((jnp.where(known, begin, 0) + spot, jnp.where(known, last.row, -last.length) + 0 * spot))
    offset = jnp.concatenate([offset] + [side[0] for side in sides])
    length = jnp.concatenate([length, jnp.full((2 * blocks * HALO_CH,), last.length, jnp.int32)])
    row = jnp.concatenate([row] + [side[1] for side in sides])
    behind = 2 * offset > length
    target = row + jnp.where(behind, length - offset, offset)
    return target[None], jnp.where(behind, -1.0, 1.0).astype(f32)[None]


def body(frames, link_to_wire, neighbours, kernel, wide_filter, tight_filter, roi_mask):
    frames, roi_mask = frames[0], roi_mask[0]
    share, ticks = frames.shape
    blocks = lax.axis_size("chan")
    detectors = lax.axis_size("apa")
    harmonics = kernel.shape[1]
    padded = max(harmonics, lane // 2)
    width = 2 * padded
    here = lax.axis_index("chan")
    detector = lax.axis_index("apa")
    lower, upper = neighbours[0, 0], neighbours[0, 1]
    head, tail = PU + PV, CHANNELS - HALO_CH
    to_next = jnp.where(upper == detector + 1, tail, head)
    to_before = jnp.where(lower == detector - 1, head, tail)
    where = jnp.stack([here, to_next, to_before]).astype(jnp.int32)
    table = jnp.asarray(forward_tables(ticks, blocks, padded))

    far = call(
        functools.partial(far_spectra, blocks), [((share, width), bf16)] * (blocks - 1),
        [scalars, whole, whole], "far_spectra",
    )(where, frames, table)
    received = [
        lax.ppermute(part, "chan", [(i, (i + s) % blocks) for i in range(blocks)])
        for s, part in enumerate(far, 1)
    ]
    wires = link_to_wire.reshape(blocks, share)
    wires = jnp.concatenate([wires[(here - s) % blocks] for s in range(blocks)])
    own, *bands = call(
        functools.partial(near_spectra, blocks),
        [((share, width), bf16)] + [((HALO_CH, width), bf16)] * (2 * blocks),
        [scalars, whole, whole, whole], "near_spectra",
    )(where, frames, table, wires[None, :share])
    halo = []
    for way, step in enumerate((1, -1)):
        for s in range(blocks):
            pairs = [
                (a * blocks + i, (a + step) * blocks + (i + s) % blocks)
                for a in range(detectors) if 0 <= a + step < detectors
                for i in range(blocks)
            ]
            halo.append(lax.ppermute(bands[way * blocks + s], ("apa", "chan"), pairs))
    targets, signs = fold_targets(wires, lower, upper, detector, blocks)
    sums, diffs, folded = call(
        functools.partial(prepare, share),
        [((all_rows, width), f32)] * 2 + [((all_rows, 2 * width), f32)],
        [whole] * 4, "prepare",
    )(kernel, targets, signs, own)
    narrow = jnp.asarray(channel_tables(planes[0].length, planes[0].rows))
    wide = jnp.asarray(channel_tables(planes[2].length, planes[2].rows))
    own, *sends = call(
        functools.partial(channel_stage, blocks, share),
        [((share, width), f32)] + [((share, width), bf16)] * (blocks - 1),
        [scalars] + [whole] * (3 * blocks + 6), "channel_stage",
        [pltpu.VMEM((CHANNELS, width), f32)],
    )(where, *received, *halo, targets, signs, folded, sums, diffs, narrow, wide)
    returned = [
        lax.ppermute(part, "chan", [(i, (i + s) % blocks) for i in range(blocks)])
        for s, part in enumerate(sends, 1)
    ]

    def in_rows(gain):
        parts = jnp.pad(gain.reshape(blocks, harmonics), ((0, 0), (0, padded - harmonics)))
        return jnp.concatenate([parts, parts], axis=1)[:, :, None]

    inverse = jnp.asarray(inverse_tables(ticks, blocks, padded))
    basis = jnp.concatenate([inverse * in_rows(wide_filter), inverse * in_rows(tight_filter)], axis=2)
    signal, bases = call(
        functools.partial(own_signal, blocks),
        [((share, ticks), f32), ((max(blocks - 1, 1), 2 * width, 2 * ticks), bf16)],
        [scalars] + [whole] * 3, "own_signal",
    )(where, own, basis, roi_mask)
    (out,) = call(
        functools.partial(whole_signal, blocks), [((share, ticks), f32)],
        [whole] * (blocks + 2), "whole_signal",
    )(signal, bases, roi_mask, *returned)
    return out[None]


def solution(mesh):
    placed = (
        P("apa", "chan", None),
        P("apa", None),
        P("apa", None),
        P(None, "chan", None),
        P(),
        P(),
        P("apa", "chan", None),
    )
    return jax.shard_map(
        body, mesh=mesh, in_specs=placed, out_specs=P("apa", "chan", None), check_vma=False
    )
```

```python
import functools
import math

import jax
import jax.numpy as jnp
import ml_dtypes
import numpy as np
from jax import lax
from jax.experimental import pallas as pl
from jax.experimental.pallas import tpu as pltpu
from jax.sharding import PartitionSpec as P

PU = 800
PV = 800
PW = 960
HALO_CH = 128
BC = 16
BT = 64
CHANNELS = 2560

two_pi = 2.0 * math.pi
lane = 128
f32 = jnp.float32
bf16 = jnp.bfloat16
whole = pl.BlockSpec(memory_space=pltpu.VMEM)
scalars = pl.BlockSpec(memory_space=pltpu.SMEM)
pinned = pl.BlockSpec(memory_space=pltpu.HBM)


def near(array):
    return pltpu.with_memory_space_constraint(array, pltpu.VMEM)


def distant(array):
    return pltpu.with_memory_space_constraint(array, pltpu.HBM)


def ceil_to(size, step):
    return -(-size // step) * step


class Plane:
    def __init__(self, length, wire, count, keep, kernel_start, row):
        self.length, self.wire, self.count, self.keep = length, wire, count, keep
        self.kernel_start, self.row = kernel_start, row
        self.half = length // 2
        self.rows = ceil_to(self.half + 1, 16)


def make_planes():
    found, row, start = [], 0, 0
    for length, wire, count, keep in (
        (PU, 0, PU, 0),
        (PV, PU, PV, 0),
        (PW + 2 * HALO_CH, PU + PV, PW, HALO_CH),
    ):
        found.append(Plane(length, wire, count, keep, start, row))
        row += found[-1].rows
        start += length
    return found


planes = make_planes()
all_rows = planes[-1].row + planes[-1].rows


def split(values):
    high = values.astype(bf16)
    return high, (values - high.astype(f32)).astype(bf16)


def channel_tables(length, rows):
    index = np.arange(rows)
    angles = (index[:, None] * index[None, :] % length) * (two_pi / length)
    inside = (index <= length // 2).astype(np.float64)
    mask = inside[:, None] * inside[None, :]
    parts = []
    for values in (np.cos(angles) * mask, np.sin(angles) * mask):
        high = values.astype(np.float32).astype(ml_dtypes.bfloat16)
        parts += [high, (values - high.astype(np.float64)).astype(np.float32).astype(ml_dtypes.bfloat16)]
    return np.stack(parts)


def tick_angles(ticks):
    return (np.arange(ticks)[:, None] * np.arange(ticks // 2)[None, :] % ticks) * (two_pi / ticks)


def in_blocks(values, blocks, padded):
    parts = np.stack(np.split(values, blocks, axis=-1))
    return np.pad(parts, [(0, 0)] * (parts.ndim - 1) + [(0, padded - parts.shape[-1])])


def forward_tables(ticks, blocks, padded):
    angles = tick_angles(ticks)
    halves = [in_blocks(part, blocks, padded) for part in (np.cos(angles), -np.sin(angles))]
    return np.concatenate(halves, axis=-1).astype(np.float32).astype(ml_dtypes.bfloat16)


def inverse_tables(ticks, blocks, padded):
    angles = tick_angles(ticks)
    weights = np.where(np.arange(ticks // 2) == 0, 1.0, 2.0) / ticks
    halves = [in_blocks(part * weights, blocks, padded) for part in (np.cos(angles), -np.sin(angles))]
    return np.ascontiguousarray(np.swapaxes(np.concatenate(halves, axis=-1), 1, 2)).astype(np.float32)


def dot(left, right):
    return jnp.dot(left, right, preferred_element_type=f32)


def one_hot(rows, first, targets):
    numbers = lax.broadcasted_iota(jnp.int32, (rows, targets.shape[1]), 0) + first
    return jnp.where(numbers == targets, 1.0, 0.0).astype(bf16)


def far_spectra(blocks, where, frames, table, *refs):
    outs, (rows, columns, sems) = refs[: blocks - 1], refs[blocks - 1 :]
    parts = 4
    size = frames.shape[0] // parts
    loads = [pltpu.make_async_copy(table, columns, sems.at[parts])]
    spans = [pl.ds(i * size, size) for i in range(parts)]
    reads = [pltpu.make_async_copy(frames.at[span], rows.at[span], sems.at[i]) for i, span in enumerate(spans)]
    for copy in loads + reads:
        copy.start()
    for copy in loads:
        copy.wait()
    for copy, span in zip(reads, spans):
        copy.wait()
        for s, out in enumerate(outs, 1):
            out[span, :] = dot(rows[span, :], columns[lax.rem(where[0] + s, blocks)]).astype(bf16)


def wires_of(wires, block, share):
    if wires.shape[0] > 1:
        return wires[pl.ds(block, 1), :]
    return wires[:, pl.ds(pl.multiple_of(block * share, lane), share)]


def edge_bands(blocks, where, neighbours, frames, table, wires, *bands):
    mine = wires_of(wires, where[0], frames.shape[0])
    head, tail = PU + PV, CHANNELS - HALO_CH
    to_next = jnp.where(neighbours[0, 1] == where[1] + 1, tail, head)
    to_before = jnp.where(neighbours[0, 0] == where[1] - 1, head, tail)
    for first, out in zip((to_next, to_before), bands):
        rows = dot(one_hot(HALO_CH, first, mine), frames[...]).astype(bf16)
        for s in range(blocks):
            spectra = dot(rows, table[lax.rem(where[0] + s, blocks)])
            out[s * HALO_CH : (s + 1) * HALO_CH, :] = spectra.astype(bf16)


def rotated(values):
    half = values.shape[1] // 2
    first = lax.broadcasted_iota(jnp.int32, values.shape, 1) < half
    turned = pltpu.roll(values, half, 1)
    return jnp.where(first, turned, -turned)


def fold_of(offset, length, row):
    behind = 2 * offset > length
    return row + jnp.where(behind, length - offset, offset), jnp.where(behind, -1.0, 1.0)


def fold_of_wires(wires):
    first, second = wires < PU, wires < PU + PV
    offset = jnp.where(first, wires, jnp.where(second, wires - PU, wires - (PU + PV) + HALO_CH))
    length = jnp.where(first, PU, jnp.where(second, PV, planes[2].length))
    row = jnp.where(first, planes[0].row, jnp.where(second, planes[1].row, planes[2].row))
    return fold_of(offset, length, row)


def fold_of_halo(begin):
    offset = lax.broadcasted_iota(jnp.int32, (1, HALO_CH), 1) + begin
    return fold_of(offset, planes[2].length, planes[2].row)


def sign_columns(signs, width):
    return jnp.transpose(jnp.broadcast_to(signs, (width, signs.shape[1])))


def fold_operand(spectra, signs):
    turned = rotated(spectra.astype(f32)) * sign_columns(signs, spectra.shape[1])
    return jnp.concatenate([spectra, turned.astype(bf16)], axis=1)


def prepare(blocks, where, kernel_source, wires, frames, table, *refs):
    sources, (sums, diffs, folded), kept = refs[:2], refs[2:5], refs[5:7]
    kernel, sems = refs[7:]
    harmonics, width = kernel.shape[1], sums.shape[1]
    kernel_copy = pltpu.make_async_copy(kernel_source, kernel, sems.at[0])
    kernel_copy.start()
    copies = [pltpu.make_async_copy(sources[i], kept[i], sems.at[1 + i]) for i in range(2)]
    for copy in copies:
        copy.start()
    spare = width // 2 - harmonics
    targets, signs = fold_of_wires(wires_of(wires, where[0], frames.shape[0]))
    spectra = dot(frames[...], table[where[0]])
    turned = rotated(spectra) * sign_columns(signs, width)
    operand = jnp.concatenate(split(spectra) + split(turned), axis=1)
    for plane in planes:
        rows = pl.ds(plane.row, plane.rows)
        both = dot(one_hot(plane.rows, plane.row, targets), operand)
        folded[rows, :width] = both[:, :width] + both[:, width : 2 * width]
        folded[rows, width:] = both[:, 2 * width : 3 * width] + both[:, 3 * width :]
    kernel_copy.wait()
    for plane in planes:
        rows = pl.ds(plane.row, plane.rows)
        start = plane.kernel_start // lane * lane
        stop = ceil_to(plane.kernel_start + plane.length, lane)
        offset = plane.kernel_start - start
        parts = []
        for z in range(2):
            parts.append(kernel[z, :, start:stop])
            if spare:
                parts.append(jnp.zeros((spare, stop - start), f32))
        values = jnp.concatenate(parts, axis=0)
        direct = jnp.transpose(values[:, : ceil_to(offset + plane.rows, lane)])[offset : offset + plane.rows]
        row = lax.broadcasted_iota(jnp.int32, (plane.rows, 1), 0)
        source = jnp.where((row > 0) & (row < plane.half), plane.length - row + offset, -1)
        column = lax.broadcasted_iota(jnp.int32, (plane.rows, stop - start), 1)
        matrix = jnp.where(column == source, 1.0, 0.0).astype(bf16)
        both = lax.dot_general(
            matrix, jnp.concatenate(split(values), axis=0), (((1,), (1,)), ((), ())), preferred_element_type=f32
        )
        mirror = (both[:, :width] + both[:, width:]) * (1.0 / plane.length)
        row = lax.broadcasted_iota(jnp.int32, (plane.rows, width), 0)
        direct = jnp.where(row <= plane.half, direct * (1.0 / plane.length), 0.0)
        sums[rows, :] = direct + mirror
        diffs[rows, :] = direct - mirror
    for copy in copies:
        copy.wait()


def two_pass(high, low, values):
    width = values.shape[1]
    joined = jnp.concatenate(split(values), axis=1)
    both = dot(high, joined) + dot(low, joined)
    return both[:, :width] + both[:, width:]


def times(values, factor):
    half = values.shape[1] // 2
    first = lax.broadcasted_iota(jnp.int32, values.shape, 1) < half
    other = pltpu.roll(factor, half, 1)
    real = jnp.where(first, factor, other)
    imag = jnp.where(first, other, factor)
    return values * real - rotated(values) * imag


def far_operand(blocks, share, where, wires, received):
    targets, signs = [], []
    for s in range(1, blocks):
        target, sign = fold_of_wires(wires_of(wires, lax.rem(where[0] + blocks - s, blocks), share))
        targets.append(target)
        signs.append(sign)
    operand = fold_operand(jnp.concatenate([ref[...] for ref in received], axis=0), jnp.concatenate(signs, axis=1))
    return jnp.concatenate(targets, axis=1), operand


def halo_operand(blocks, where, neighbours, halo):
    bands, targets, signs = [], [], []
    lower, upper = neighbours[0, 0], neighbours[0, 1]
    never = -4 * planes[2].length
    for way in range(2):
        total = halo[way][:HALO_CH, :].astype(f32)
        for ref in halo[2:]:
            total += ref[way * HALO_CH : (way + 1) * HALO_CH, :].astype(f32)
        bands.append(total.astype(bf16))
        other = where[1] + 2 * way - 1
        begin = jnp.where(upper == other, planes[2].length - HALO_CH, never)
        begin = jnp.where(lower == other, 0, begin)
        target, sign = fold_of_halo(jnp.where(other < 0, never, begin))
        targets.append(target)
        signs.append(sign)
    operand = fold_operand(jnp.concatenate(bands, axis=0), jnp.concatenate(signs, axis=1))
    return jnp.concatenate(targets, axis=1), operand


def plane_result(plane, far, halo, folded, sums, diffs, table):
    rows = pl.ds(plane.row, plane.rows)
    both = folded[rows, :] + dot(one_hot(plane.rows, plane.row, far[0]), far[1])
    if plane.keep:
        both += dot(one_hot(plane.rows, plane.row, halo[0]), halo[1])
    width = both.shape[1] // 2
    even = two_pass(table[0], table[1], both[:, :width])
    odd = two_pass(table[2], table[3], both[:, width:])
    plus, minus = sums[rows, :], diffs[rows, :]
    total = times(even, plus) + times(odd, minus)
    gap = times(even, minus) + times(odd, plus)
    kept = slice(plane.keep, plane.rows)
    cosine = two_pass(table[0, kept], table[1, kept], total)
    sine = two_pass(table[2, kept], table[3, kept], -rotated(gap))
    straight = plane.count // 2
    back = jnp.concatenate(split(cosine - sine), axis=1)
    row = lax.broadcasted_iota(jnp.int32, (straight, back.shape[0]), 0)
    column = lax.broadcasted_iota(jnp.int32, (straight, back.shape[0]), 1) + plane.keep
    turned = dot(jnp.where(column == plane.half - row, 1.0, 0.0).astype(bf16), back)
    return (cosine + sine)[:straight], turned[:, :width] + turned[:, width:]


def put(result, plane, *operands):
    lower, upper = plane_result(plane, *operands)
    result[: plane.count // 2, :] = lower
    result[plane.count // 2 : plane.count, :] = upper


def all_planes(blocks, share, where, neighbours, *refs):
    received, halo = refs[: blocks - 1], refs[blocks - 1 : 2 * blocks]
    wires, folded, sums, diffs, narrow, wide, own = refs[2 * blocks : 2 * blocks + 7]
    sends, result = refs[2 * blocks + 7 : 3 * blocks + 6], refs[3 * blocks + 6]
    far = far_operand(blocks, share, where, wires, received)
    bands = halo_operand(blocks, where, neighbours, halo)
    for plane in planes:
        operands = (far, bands, folded, sums, diffs, wide if plane.keep else narrow)
        put(result.at[pl.ds(plane.wire, plane.count)], plane, *operands)
    here = where[0]
    own[...] = result[pl.ds(pl.multiple_of(here * share, share), share), :]
    for shift, out in enumerate(sends, 1):
        first = pl.multiple_of(lax.rem(here + shift, blocks) * share, share)
        out[...] = result[pl.ds(first, share), :].astype(bf16)


def middle_plane(share, where, far, wires, folded, sums, diffs, narrow, send, own, result):
    middle = planes[1]
    operand = far_operand(2, share, where, wires, [far])
    put(result, middle, operand, None, folded, sums, diffs, narrow)
    below = share - middle.wire
    above = middle.count - below

    @pl.when(where[0] == 0)
    def _():
        send[:above, :] = result[below:, :].astype(bf16)
        send[above:, :] = jnp.zeros((below - above, send.shape[1]), bf16)
        own[...] = result[:below, :]

    @pl.when(where[0] != 0)
    def _():
        send[...] = result[:below, :].astype(bf16)
        own[:above, :] = result[below:, :]
        own[above:, :] = jnp.zeros((below - above, own.shape[1]), f32)


def outer_plane(share, where, neighbours, far, halo0, halo1, halo2, wires, folded, sums, diffs, narrow, wide, send, result):
    first, _, last = planes
    operand = far_operand(2, share, where, wires, [far])

    @pl.when(where[0] == 0)
    def _():
        bands = halo_operand(2, where, neighbours, (halo0, halo1, halo2))
        put(result, last, operand, bands, folded, sums, diffs, wide)
        send[...] = result[...].astype(bf16)

    @pl.when(where[0] != 0)
    def _():
        put(result, first, operand, None, folded, sums, diffs, narrow)
        send[: first.count, :] = result[: first.count, :].astype(bf16)
        send[first.count :, :] = jnp.zeros((last.count - first.count, send.shape[1]), bf16)


def own_planes(share, where, neighbours, far, halo0, halo1, halo2, wires, folded, sums, diffs, narrow, wide, part, basis,
               wide_filter, tight_filter, mask, signal, bases, inside, result, basis_room, sem):
    first, middle, last = planes
    basis_copy = pltpu.make_async_copy(basis, basis_room, sem)
    basis_copy.start()
    operand = far_operand(2, share, where, wires, [far])
    above = middle.count - (share - middle.wire)

    @pl.when(where[0] == 0)
    def _():
        put(result, first, operand, None, folded, sums, diffs, narrow)
        result[first.count :, :] = part[...]

    @pl.when(where[0] != 0)
    def _():
        bands = halo_operand(2, where, neighbours, (halo0, halo1, halo2))
        put(result.at[pl.ds(above, last.count)], last, operand, bands, folded, sums, diffs, wide)
        result[:above, :] = part[:above, :]

    basis_copy.wait()
    own_signal(2, where, result, basis_room, wide_filter, tight_filter, mask, signal, bases, inside)


def spread_mask(mask, share, ticks):
    marked = jnp.where(mask == 1, 1.0, 0.0).astype(bf16)
    row = lax.broadcasted_iota(jnp.int32, (share, mask.shape[1]), 0)
    column = lax.broadcasted_iota(jnp.int32, (share, mask.shape[1]), 1)
    taken = jnp.where(row // BC == column, 1.0, 0.0).astype(bf16)
    rows = lax.dot_general(taken, marked, (((1,), (1,)), ((), ())), preferred_element_type=f32).astype(bf16)
    row = lax.broadcasted_iota(jnp.int32, (mask.shape[0], ticks), 0)
    column = lax.broadcasted_iota(jnp.int32, (mask.shape[0], ticks), 1)
    return dot(rows, jnp.where(column // BT == row, 1.0, 0.0).astype(bf16))


def chosen_signal(both, inside):
    ticks = inside.shape[1]
    return jnp.where(inside > 0.5, both[:, :ticks], both[:, ticks:])


def scaled_basis(block, blocks, basis, filters, harmonics):
    padded = basis.shape[1] // 2
    ticks = basis.shape[2]
    spread = []
    for gain in filters:
        columns = gain[...] if blocks == 1 else None
        for b in range(blocks):
            piece = gain[:, b * harmonics : (b + 1) * harmonics]
            columns = piece if columns is None else jnp.where(block == b, piece, columns)
        if padded > harmonics:
            columns = jnp.concatenate([columns, jnp.zeros((1, padded - harmonics), f32)], axis=1)
        columns = jnp.concatenate([columns, columns], axis=1)
        tall = jnp.transpose(jnp.broadcast_to(columns, (lane, 2 * padded)))
        spread.append(jnp.concatenate([tall] * (ticks // lane), axis=1))
    values = basis[block]
    return split(jnp.concatenate([values * part for part in spread], axis=1))


def own_signal(blocks, where, own, basis, wide_filter, tight_filter, mask, signal, bases, inside):
    here = where[0]
    ticks = signal.shape[1]
    harmonics = wide_filter.shape[1] // blocks
    filters = (wide_filter, tight_filter)
    high, low = scaled_basis(here, blocks, basis, filters, harmonics)
    joined = jnp.concatenate(split(own[...]), axis=1)
    both = dot(joined, jnp.concatenate([high, high], axis=0))
    both += dot(joined, jnp.concatenate([low, low], axis=0))
    inside[...] = spread_mask(mask[...], own.shape[0], ticks)
    signal[...] = chosen_signal(both, inside[...])
    for shift in range(1, blocks):
        parts = scaled_basis(lax.rem(here + blocks - shift, blocks), blocks, basis, filters, harmonics)
        bases[shift - 1] = jnp.concatenate(parts, axis=0)


def whole_signal(blocks, signal, bases, inside, *refs):
    out = refs[-1]
    both = None
    for shift in range(1, blocks):
        values = refs[shift - 1][...]
        term = dot(jnp.concatenate([values, values], axis=1), bases[shift - 1])
        both = term if both is None else both + term
    if both is None:
        out[...] = signal[...]
    else:
        out[...] = signal[...] + chosen_signal(both, inside[...])


def part_signal(spans, where, signal, bases, inside, values, *refs):
    out, room, sems = refs[-3:]
    step = room.shape[0] // sems.shape[0]
    for device, (first, count) in enumerate(spans):

        @pl.when(where[0] == device)
        def _(first=first, count=count):
            copies = []
            for i in range(count // step):
                some = values[i * step : (i + 1) * step, :]
                both = dot(jnp.concatenate([some, some], axis=1), bases[0])
                rows, slot = pl.ds(first + i * step, step), pl.ds(i * step, step)
                room[slot, :] = signal[rows, :] + chosen_signal(both, inside[rows, :])
                copies.append(pltpu.make_async_copy(room.at[slot], out.at[rows], sems.at[i]))
                copies[-1].start()
            for copy in copies:
                copy.wait()


def call(kernel, outs, ins, name, scratch=(), final=False, aliases=None):
    kind = jax.ShapeDtypeStruct if final else pltpu.VMEM
    return pl.pallas_call(
        kernel,
        out_shape=[kind(shape, dtype) for shape, dtype in outs],
        in_specs=ins,
        out_specs=[pinned if final else whole] * len(outs),
        scratch_shapes=scratch,
        compiler_params=pltpu.CompilerParams(vmem_limit_bytes=28 * 1024 * 1024),
        cost_estimate=pl.CostEstimate(flops=0, bytes_accessed=0, transcendentals=0),
        input_output_aliases=aliases or {},
        name=name,
    )


def body(frames, link_to_wire, neighbours, kernel, wide_filter, tight_filter, roi_mask):
    frames, roi_mask = frames[0], roi_mask[0]
    share, ticks = frames.shape
    blocks = lax.axis_size("chan")
    detectors = lax.axis_size("apa")
    padded = max(kernel.shape[1], lane // 2)
    width = 2 * padded
    here = lax.axis_index("chan")
    detector = lax.axis_index("apa")
    where = jnp.stack([here, detector]).astype(jnp.int32)
    wires = link_to_wire if share % lane == 0 else link_to_wire.reshape(blocks, share)
    table = jnp.asarray(forward_tables(ticks, blocks, padded))

    def around(parts):
        return [
            near(lax.ppermute(part, "chan", [(i, (i + s) % blocks) for i in range(blocks)]))
            for s, part in enumerate(parts, 1)
        ]

    *far, frames, table = call(
        functools.partial(far_spectra, blocks),
        [((share, width), bf16)] * (blocks - 1) + [((share, ticks), bf16), ((blocks, ticks, width), bf16)],
        [scalars, pinned, pinned], "far_spectra", [pltpu.SemaphoreType.DMA((5,))],
    )(where, distant(frames), distant(table))
    frames, table = near(frames), near(table)
    received = around(far)
    bands = call(
        functools.partial(edge_bands, blocks), [((blocks * HALO_CH, width), bf16)] * 2,
        [scalars] * 2 + [whole] * 3, "edge_bands",
    )(where, neighbours, frames, table, wires)
    halo = []
    for step, band in zip((1, -1), bands):
        pairs = [(a, a + step) for a in range(detectors) if 0 <= a + step < detectors]
        halo.append(lax.ppermute(band, "apa", pairs))
    shares = [
        jnp.concatenate([band[s * HALO_CH : (s + 1) * HALO_CH] for band in halo]) for s in range(1, blocks)
    ]
    halo = [near(band) for band in halo] + around(shares)
    tables = [channel_tables(planes[i].length, planes[i].rows) for i in (0, 2)]
    ready = call(
        functools.partial(prepare, blocks),
        [((all_rows, width), f32)] * 2 + [((all_rows, 2 * width), f32)] + [(part.shape, bf16) for part in tables],
        [scalars, pinned] + [whole] * 3 + [pinned] * 2, "prepare",
        [pltpu.VMEM(kernel.shape, f32), pltpu.SemaphoreType.DMA((3,))],
    )(where, distant(kernel), wires, frames, table, *(distant(jnp.asarray(part)) for part in tables))
    sums, diffs, folded, narrow, wide = map(near, ready)
    basis = jnp.asarray(inverse_tables(ticks, blocks, padded))
    basis_room = pltpu.VMEM(basis.shape, f32)
    filters = (wide_filter[None], tight_filter[None])
    mask = jnp.transpose(roi_mask)
    signal_shapes = [
        ((share, ticks), f32), ((max(blocks - 1, 1), 2 * width, 2 * ticks), bf16), ((share, ticks), f32)
    ]
    if blocks != 2:
        own, *sends = call(
            functools.partial(all_planes, blocks, share),
            [((share, width), f32)] + [((share, width), bf16)] * (blocks - 1),
            [scalars] * 2 + [whole] * (2 * blocks + 6), "all_planes",
            [pltpu.VMEM((CHANNELS, width), f32)],
        )(where, neighbours, *received, *halo, wires, folded, sums, diffs, narrow, wide)
        returned = around(sends)
        signal, bases, inside = call(
            functools.partial(own_signal, blocks), signal_shapes,
            [scalars] + [whole] * 5, "own_signal",
        )(where, near(own), basis, *filters, mask)
        out = pl.pallas_call(
            functools.partial(whole_signal, blocks),
            out_shape=jax.ShapeDtypeStruct((share, ticks), f32),
            in_specs=[whole] * (blocks + 2),
            out_specs=whole,
            name="whole_signal",
        )(near(signal), near(bases), near(inside), *returned)
        return out[None]

    below, above = share - PU, PU + PV - share
    sent, part = call(
        functools.partial(middle_plane, share), [((below, width), bf16), ((below, width), f32)],
        [scalars] + [whole] * 6, "middle_plane", [pltpu.VMEM((PV, width), f32)],
    )(where, *received, wires, folded, sums, diffs, narrow)
    (early,) = around([sent])
    (sent,) = call(
        functools.partial(outer_plane, share), [((PW, width), bf16)],
        [scalars] * 2 + [whole] * 10, "outer_plane", [pltpu.VMEM((PW, width), f32)],
    )(where, neighbours, *received, *halo, wires, folded, sums, diffs, narrow, wide)
    (late,) = around([sent])
    ready = call(
        functools.partial(own_planes, share), signal_shapes,
        [scalars] * 2 + [whole] * 11 + [pinned] + [whole] * 3, "own_planes",
        [pltpu.VMEM((share, width), f32), basis_room, pltpu.SemaphoreType.DMA],
    )(where, neighbours, *received, *halo, wires, folded, sums, diffs, narrow, wide, near(part), distant(basis), *filters, mask)
    signal, bases, inside = map(near, ready)

    def finish(values, spans, *before):
        step = math.gcd(*(count for _, count in spans))
        rows = max(count for _, count in spans)
        (out,) = call(
            functools.partial(part_signal, spans), [((share, ticks), f32)],
            [scalars] + [whole] * 4 + [pinned] * len(before), "part_signal",
            [pltpu.VMEM((rows, ticks), f32), pltpu.SemaphoreType.DMA((rows // step,))],
            final=True, aliases={5: 0} if before else None,
        )(where, signal, bases, inside, values, *before)
        return out

    out = finish(early, ((PU, below), (0, above)))
    return finish(late, ((0, PU), (above, PW)), out)[None]


def solution(mesh):
    placed = (
        P("apa", "chan", None),
        P("apa", None),
        P("apa", None),
        P(None, "chan", None),
        P(),
        P(),
        P("apa", "chan", None),
    )
    return jax.shard_map(
        body, mesh=mesh, in_specs=placed, out_specs=P("apa", "chan", None), check_vma=False
    )
```

```python
import functools
import math

import jax
import jax.numpy as jnp
import ml_dtypes
import numpy as np
from jax import lax
from jax.experimental import pallas as pl
from jax.experimental.pallas import tpu as pltpu
from jax.sharding import PartitionSpec as P

PU = 800
PV = 800
PW = 960
HALO_CH = 128
BC = 16
BT = 64
CHANNELS = 2560

two_pi = 2.0 * math.pi
lane = 128
f32 = jnp.float32
bf16 = jnp.bfloat16
whole = pl.BlockSpec(memory_space=pltpu.VMEM)
pinned = pl.BlockSpec(memory_space=pltpu.HBM)


def near(array):
    return pltpu.with_memory_space_constraint(array, pltpu.VMEM)


def distant(array):
    return pltpu.with_memory_space_constraint(array, pltpu.HBM)


def ceil_to(size, step):
    return -(-size // step) * step


class Plane:
    def __init__(self, length, wire, count, keep, kernel_start, row):
        self.length, self.wire, self.count, self.keep = length, wire, count, keep
        self.kernel_start, self.row = kernel_start, row
        self.half = length // 2
        self.rows = ceil_to(self.half + 1, 16)


def make_planes():
    found, row, start = [], 0, 0
    for length, wire, count, keep in (
        (PU, 0, PU, 0),
        (PV, PU, PV, 0),
        (PW + 2 * HALO_CH, PU + PV, PW, HALO_CH),
    ):
        found.append(Plane(length, wire, count, keep, start, row))
        row += found[-1].rows
        start += length
    return found


planes = make_planes()
all_rows = planes[-1].row + planes[-1].rows


def split(values):
    high = values.astype(bf16)
    return high, (values - high.astype(f32)).astype(bf16)


def channel_tables(length, rows, order):
    index = np.arange(rows)
    angles = (index[:, None] * index[None, :] % length) * (two_pi / length)
    inside = (index <= length // 2).astype(np.float64)
    mask = inside[:, None] * inside[None, :]
    found = []
    for values in (np.cos(angles) * mask, np.sin(angles) * mask):
        high = values.astype(np.float32).astype(ml_dtypes.bfloat16)
        low = (values - high.astype(np.float64)).astype(np.float32).astype(ml_dtypes.bfloat16)
        found.append(np.concatenate([(high, low)[i] for i in order], axis=1))
    return np.stack(found)


def tick_angles(ticks):
    return (np.arange(ticks)[:, None] * np.arange(ticks // 2)[None, :] % ticks) * (two_pi / ticks)


def in_blocks(values, blocks, padded):
    parts = np.stack(np.split(values, blocks, axis=-1))
    return np.pad(parts, [(0, 0)] * (parts.ndim - 1) + [(0, padded - parts.shape[-1])])


def forward_tables(ticks, blocks, padded):
    angles = tick_angles(ticks)
    halves = [in_blocks(part, blocks, padded) for part in (np.cos(angles), -np.sin(angles))]
    return np.concatenate(halves, axis=-1).astype(np.float32).astype(ml_dtypes.bfloat16)


def inverse_tables(ticks, blocks, padded):
    angles = tick_angles(ticks)
    weights = np.where(np.arange(ticks // 2) == 0, 1.0, 2.0) / ticks
    halves = [in_blocks(part * weights, blocks, padded) for part in (np.cos(angles), -np.sin(angles))]
    return np.ascontiguousarray(np.swapaxes(np.concatenate(halves, axis=-1), 1, 2)).astype(np.float32)


def dot(left, right):
    return jnp.dot(left, right, preferred_element_type=f32)


def one_hot(rows, first, targets):
    numbers = lax.broadcasted_iota(jnp.int32, (rows, targets.shape[1]), 0) + first
    return jnp.where(numbers == targets, 1.0, 0.0).astype(bf16)


def wires_of(wires, block, share):
    if wires.shape[0] > 1:
        return wires[pl.ds(block, 1), :]
    return wires[:, pl.ds(pl.multiple_of(block * share, lane), share)]


def tick_spectra(blocks, frames_source, table_source, wires_source, neighbours_source, *refs):
    outs, bands, (frames, table, wires, neighbours) = refs[: blocks - 1], refs[blocks - 1 : blocks + 1], refs[blocks + 1 : blocks + 5]
    (sems,) = refs[blocks + 5 :]
    here, detector = lax.axis_index("chan"), lax.axis_index("apa")
    parts = 4
    size = frames.shape[0] // parts
    spans = [pl.ds(i * size, size) for i in range(parts)]
    pairs = [(table_source, table), (wires_source, wires), (neighbours_source, neighbours)]
    pairs += [(frames_source.at[span], frames.at[span]) for span in spans]
    copies = [pltpu.make_async_copy(source, target, sems.at[i]) for i, (source, target) in enumerate(pairs)]
    for copy in copies:
        copy.start()
    copies[0].wait()
    for copy, span in zip(copies[3:], spans):
        copy.wait()
        for s, out in enumerate(outs, 1):
            out[span, :] = dot(frames[span, :], table[lax.rem(here + s, blocks)]).astype(bf16)
    for copy in copies[1:3]:
        copy.wait()
    mine = wires_of(wires, here, frames.shape[0])
    head, tail = PU + PV, CHANNELS - HALO_CH
    to_next = jnp.where(neighbours[:, 1:2] == detector + 1, tail, head)
    to_before = jnp.where(neighbours[:, 0:1] == detector - 1, head, tail)
    for first, out in zip((to_next, to_before), bands):
        rows = dot(one_hot(HALO_CH, first, mine), frames[...]).astype(bf16)
        for s in range(blocks):
            spectra = dot(rows, table[lax.rem(here + s, blocks)])
            out[s * HALO_CH : (s + 1) * HALO_CH, :] = spectra.astype(bf16)


def lane_signs(width):
    return jnp.where(lax.broadcasted_iota(jnp.int32, (1, width), 1) < width // 2, 1.0, -1.0)


def rotated(values):
    width = values.shape[1]
    return pltpu.roll(values, width // 2, 1) * lane_signs(width)


def spread(values):
    width = values.shape[1]
    first = lax.broadcasted_iota(jnp.int32, values.shape, 1) < width // 2
    other = pltpu.roll(values, width // 2, 1)
    return jnp.concatenate([jnp.where(first, values, other), jnp.where(first, other, values)], axis=1)


def fold_of(offset, length, row):
    behind = 2 * offset > length
    return row + jnp.where(behind, length - offset, offset), jnp.where(behind, -1.0, 1.0)


def fold_of_wires(wires):
    first, second = wires < PU, wires < PU + PV
    offset = jnp.where(first, wires, jnp.where(second, wires - PU, wires - (PU + PV) + HALO_CH))
    length = jnp.where(first, PU, jnp.where(second, PV, planes[2].length))
    row = jnp.where(first, planes[0].row, jnp.where(second, planes[1].row, planes[2].row))
    return fold_of(offset, length, row)


def fold_of_halo(begin):
    offset = lax.broadcasted_iota(jnp.int32, (1, HALO_CH), 1) + begin
    return fold_of(offset, planes[2].length, planes[2].row)


def sign_columns(signs, width):
    return jnp.transpose(jnp.broadcast_to(signs, (width, signs.shape[1])))


def fold_operand(spectra, signs):
    turned = rotated(spectra.astype(f32)) * sign_columns(signs, spectra.shape[1])
    return jnp.concatenate([spectra, turned.astype(bf16)], axis=1)


def near_part(sources, wires, frames, table, folded, *refs):
    kept, sems = refs[:-1], refs[-1]
    copies = [pltpu.make_async_copy(source, target, sems.at[i]) for i, (source, target) in enumerate(zip(sources, kept))]
    for copy in copies:
        copy.start()
    here = lax.axis_index("chan")
    width = folded.shape[1] // 2
    targets, signs = fold_of_wires(wires_of(wires, here, frames.shape[0]))
    spectra = dot(frames[...], table[here])
    turned = rotated(spectra) * sign_columns(signs, width)
    operand = jnp.concatenate(split(spectra) + split(turned), axis=1)
    for plane in planes:
        rows = pl.ds(plane.row, plane.rows)
        both = dot(one_hot(plane.rows, plane.row, targets), operand)
        folded[rows, :width] = both[:, :width] + both[:, width : 2 * width]
        folded[rows, width:] = both[:, 2 * width : 3 * width] + both[:, 3 * width :]
    for copy in copies:
        copy.wait()


def kernel_factors(kernel, sums, diffs):
    harmonics, width = kernel.shape[1], sums.shape[1] // 2
    spare = width // 2 - harmonics
    for plane in planes:
        rows = pl.ds(plane.row, plane.rows)
        start = plane.kernel_start // lane * lane
        stop = ceil_to(plane.kernel_start + plane.length, lane)
        offset = plane.kernel_start - start
        parts = []
        for z in range(2):
            parts.append(kernel[z, :, start:stop])
            if spare:
                parts.append(jnp.zeros((spare, stop - start), f32))
        values = jnp.concatenate(parts, axis=0)
        direct = jnp.transpose(values[:, : ceil_to(offset + plane.rows, lane)])[offset : offset + plane.rows]
        row = lax.broadcasted_iota(jnp.int32, (plane.rows, 1), 0)
        source = jnp.where((row > 0) & (row < plane.half), plane.length - row + offset, -1)
        column = lax.broadcasted_iota(jnp.int32, (plane.rows, stop - start), 1)
        matrix = jnp.where(column == source, 1.0, 0.0).astype(bf16)
        both = lax.dot_general(
            matrix, jnp.concatenate(split(values), axis=0), (((1,), (1,)), ((), ())), preferred_element_type=f32
        )
        mirror = (both[:, :width] + both[:, width:]) * (1.0 / plane.length)
        row = lax.broadcasted_iota(jnp.int32, (plane.rows, width), 0)
        direct = jnp.where(row <= plane.half, direct * (1.0 / plane.length), 0.0)
        sums[rows, :] = spread(direct + mirror)
        diffs[rows, :] = spread(direct - mirror)


def multiplied(even, odd, plus, minus):
    width = even.shape[1]
    even_turned, odd_turned = rotated(even), rotated(odd)
    plus_re, plus_im, minus_re, minus_im = plus[:, :width], plus[:, width:], minus[:, :width], minus[:, width:]
    total = (even * plus_re + odd * minus_re) - (even_turned * plus_im + odd_turned * minus_im)
    gap = (even * minus_im + odd * plus_im) + (even_turned * minus_re + odd_turned * plus_re)
    return total, -gap


def far_operand(blocks, share, wires, received):
    here = lax.axis_index("chan")
    targets, signs = [], []
    for s in range(1, blocks):
        target, sign = fold_of_wires(wires_of(wires, lax.rem(here + blocks - s, blocks), share))
        targets.append(target)
        signs.append(sign)
    operand = fold_operand(jnp.concatenate([ref[...] for ref in received], axis=0), jnp.concatenate(signs, axis=1))
    return jnp.concatenate(targets, axis=1), operand


def halo_operand(blocks, neighbours, halo):
    bands, targets, signs = [], [], []
    detector = lax.axis_index("apa")
    lower, upper = neighbours[:, 0:1], neighbours[:, 1:2]
    never = -4 * planes[2].length
    for way in range(2):
        total = halo[way][:HALO_CH, :].astype(f32)
        for ref in halo[2:]:
            total += ref[way * HALO_CH : (way + 1) * HALO_CH, :].astype(f32)
        bands.append(total.astype(bf16))
        other = detector + 2 * way - 1
        begin = jnp.where(upper == other, planes[2].length - HALO_CH, never)
        begin = jnp.where(lower == other, 0, begin)
        target, sign = fold_of_halo(jnp.where(other < 0, never, begin))
        targets.append(target)
        signs.append(sign)
    operand = fold_operand(jnp.concatenate(bands, axis=0), jnp.concatenate(signs, axis=1))
    return jnp.concatenate(targets, axis=1), operand


def halves(plane, cosine, sine, turned):
    straight = plane.count // 2
    width = cosine.shape[1]
    row = lax.broadcasted_iota(jnp.int32, (straight, cosine.shape[0]), 0)
    column = lax.broadcasted_iota(jnp.int32, (straight, cosine.shape[0]), 1)
    matrix = jnp.where(column == plane.half - plane.keep - row, 1.0, 0.0).astype(bf16)
    if turned:
        both = dot(matrix, jnp.concatenate(split(cosine - sine), axis=1))
        return (cosine + sine)[:straight], both[:, :width] + both[:, width:]
    high, low = split(cosine - sine)
    return (cosine + sine)[:straight], dot(matrix, high) + dot(matrix, low)


def last_plane(far, bands, folded, sums, diffs, wide):
    plane = planes[2]
    rows = pl.ds(plane.row, plane.rows)
    both = folded[rows, :] + dot(one_hot(plane.rows, plane.row, far[0]), far[1])
    both += dot(one_hot(plane.rows, plane.row, bands[0]), bands[1])
    width = both.shape[1] // 2

    def transform(table, values):
        joined = jnp.concatenate(split(values), axis=1)
        result = dot(table, jnp.concatenate([joined, joined], axis=0))
        return result[:, :width] + result[:, width:]

    even, odd = transform(wide[0], both[:, :width]), transform(wide[1], both[:, width:])
    total, gap = multiplied(even, odd, sums[rows, :], diffs[rows, :])
    cosine, sine = transform(wide[0, plane.keep :], total), transform(wide[1, plane.keep :], gap)
    return jnp.concatenate(halves(plane, cosine, sine, True), axis=0)


def first_planes(far, folded, sums, diffs, narrow):
    plane = planes[0]
    count = plane.rows
    both = folded[: 2 * count, :] + dot(one_hot(2 * count, 0, far[0]), far[1])
    width = both.shape[1] // 2

    def transform(table, values):
        high, low = split(jnp.concatenate(values, axis=1))
        return dot(table, jnp.concatenate([high, high, low], axis=0))

    even = transform(narrow[0], [both[:count, :width], both[count:, :width]])
    odd = transform(narrow[1], [both[:count, width:], both[count:, width:]])
    totals, gaps = [], []
    for i in range(2):
        rows, lanes = slice(i * count, (i + 1) * count), slice(i * width, (i + 1) * width)
        total, gap = multiplied(even[:, lanes], odd[:, lanes], sums[rows, :], diffs[rows, :])
        totals.append(total)
        gaps.append(gap)
    return halves(plane, transform(narrow[0], totals), transform(narrow[1], gaps), False)


def put_first(result, *operands):
    lower, upper = first_planes(*operands)
    width, straight = result.shape[1], lower.shape[0]
    for i in range(2):
        lanes, start = slice(i * width, (i + 1) * width), planes[i].wire
        result[start : start + straight, :] = lower[:, lanes]
        result[start + straight : start + 2 * straight, :] = upper[:, lanes]


def all_planes(blocks, share, neighbours, *refs):
    received, halo = refs[: blocks - 1], refs[blocks - 1 : 2 * blocks]
    wires, folded, sums, diffs, narrow, wide, own = refs[2 * blocks : 2 * blocks + 7]
    sends, result = refs[2 * blocks + 7 : 3 * blocks + 6], refs[3 * blocks + 6]
    far = far_operand(blocks, share, wires, received)
    bands = halo_operand(blocks, neighbours, halo)
    put_first(result, far, folded, sums, diffs, narrow)
    result[planes[2].wire :, :] = last_plane(far, bands, folded, sums, diffs, wide)
    here = lax.axis_index("chan")
    own[...] = result[pl.ds(pl.multiple_of(here * share, share), share), :]
    for shift, out in enumerate(sends, 1):
        first = pl.multiple_of(lax.rem(here + shift, blocks) * share, share)
        out[...] = result[pl.ds(first, share), :].astype(bf16)


def leading_planes(share, neighbours, far, halo0, halo1, halo2, wires, folded, sums, diffs, narrow, wide, send, rest,
                   targets, operand, result):
    targets[...], operand[...] = far_operand(2, share, wires, [far])
    count = send.shape[0]

    @pl.when(lax.axis_index("chan") == 0)
    def _():
        bands = halo_operand(2, neighbours, (halo0, halo1, halo2))
        values = last_plane((targets[...], operand[...]), bands, folded, sums, diffs, wide)
        send[...] = values.astype(bf16)
        rest[...] = jnp.zeros(rest.shape, f32)

    @pl.when(lax.axis_index("chan") != 0)
    def _():
        put_first(result, (targets[...], operand[...]), folded, sums, diffs, narrow)
        send[...] = result[:count, :].astype(bf16)
        rest[...] = result[count:, :]


def trailing_planes(share, neighbours, halo0, halo1, halo2, targets, operand, rest, folded, sums, diffs, narrow, wide,
                    send, own, result):
    more = send.shape[0]
    operands = (targets[...], operand[...])

    @pl.when(lax.axis_index("chan") == 0)
    def _():
        put_first(result, operands, folded, sums, diffs, narrow)
        own[...] = result[:share, :]
        send[...] = result[share:, :].astype(bf16)

    @pl.when(lax.axis_index("chan") != 0)
    def _():
        bands = halo_operand(2, neighbours, (halo0, halo1, halo2))
        own[more:, :] = last_plane(operands, bands, folded, sums, diffs, wide)
        own[:more, :] = rest[more:, :]
        send[...] = rest[:more, :].astype(bf16)


def spread_mask(mask, share, ticks):
    marked = jnp.where(mask == 1, 1.0, 0.0).astype(bf16)
    row = lax.broadcasted_iota(jnp.int32, (share, mask.shape[1]), 0)
    column = lax.broadcasted_iota(jnp.int32, (share, mask.shape[1]), 1)
    taken = jnp.where(row // BC == column, 1.0, 0.0).astype(bf16)
    rows = lax.dot_general(taken, marked, (((1,), (1,)), ((), ())), preferred_element_type=f32).astype(bf16)
    row = lax.broadcasted_iota(jnp.int32, (mask.shape[0], ticks), 0)
    column = lax.broadcasted_iota(jnp.int32, (mask.shape[0], ticks), 1)
    return dot(rows, jnp.where(column // BT == row, 1.0, 0.0).astype(bf16))


def chosen_signal(both, inside):
    ticks = inside.shape[1]
    return jnp.where(inside > 0.5, both[:, :ticks], both[:, ticks:])


def scaled_basis(block, blocks, basis, filters, harmonics):
    padded = basis.shape[1] // 2
    ticks = basis.shape[2]
    gains = []
    for gain in filters:
        columns = gain[...] if blocks == 1 else None
        for b in range(blocks):
            piece = gain[:, b * harmonics : (b + 1) * harmonics]
            columns = piece if columns is None else jnp.where(block == b, piece, columns)
        if padded > harmonics:
            columns = jnp.concatenate([columns, jnp.zeros((1, padded - harmonics), f32)], axis=1)
        columns = jnp.concatenate([columns, columns], axis=1)
        tall = jnp.transpose(jnp.broadcast_to(columns, (lane, 2 * padded)))
        gains.append(jnp.concatenate([tall] * (ticks // lane), axis=1))
    values = basis[block]
    return split(jnp.concatenate([values * part for part in gains], axis=1))


def own_signal(blocks, own, basis_source, wide_filter, tight_filter, mask, signal, bases, inside, basis, sem):
    basis_copy = pltpu.make_async_copy(basis_source, basis, sem)
    basis_copy.start()
    inside[...] = spread_mask(mask[...], own.shape[0], signal.shape[1])
    basis_copy.wait()
    here = lax.axis_index("chan")
    ticks = signal.shape[1]
    harmonics = wide_filter.shape[1] // blocks
    filters = (wide_filter, tight_filter)
    high, low = scaled_basis(here, blocks, basis, filters, harmonics)
    joined = jnp.concatenate(split(own[...]), axis=1)
    both = dot(joined, jnp.concatenate([high, high], axis=0))
    both += dot(joined, jnp.concatenate([low, low], axis=0))
    signal[...] = chosen_signal(both, inside[...])
    for shift in range(1, blocks):
        parts = scaled_basis(lax.rem(here + blocks - shift, blocks), blocks, basis, filters, harmonics)
        bases[shift - 1] = jnp.concatenate(parts, axis=0)


def whole_signal(blocks, signal, bases, inside, *refs):
    out = refs[-1]
    both = None
    for shift in range(1, blocks):
        values = refs[shift - 1][...]
        term = dot(jnp.concatenate([values, values], axis=1), bases[shift - 1])
        both = term if both is None else both + term
    if both is None:
        out[...] = signal[...]
    else:
        out[...] = signal[...] + chosen_signal(both, inside[...])


def part_signal(spans, signal, bases, inside, values, *refs):
    out, room, sems = refs[-3:]
    step = room.shape[0] // sems.shape[0]
    for device, (first, count) in enumerate(spans):

        @pl.when(lax.axis_index("chan") == device)
        def _(first=first, count=count):
            copies = []
            for i in range(count // step):
                some = values[i * step : (i + 1) * step, :]
                both = dot(jnp.concatenate([some, some], axis=1), bases[0])
                rows, slot = pl.ds(first + i * step, step), pl.ds(i * step, step)
                room[slot, :] = signal[rows, :] + chosen_signal(both, inside[rows, :])
                copies.append(pltpu.make_async_copy(room.at[slot], out.at[rows], sems.at[i]))
                copies[-1].start()
            for copy in copies:
                copy.wait()


def call(kernel, outs, ins, name, scratch=(), final=False, aliases=None):
    kind = jax.ShapeDtypeStruct if final else pltpu.VMEM
    return pl.pallas_call(
        kernel,
        out_shape=[kind(shape, dtype) for shape, dtype in outs],
        in_specs=ins,
        out_specs=[pinned if final else whole] * len(outs),
        scratch_shapes=scratch,
        compiler_params=pltpu.CompilerParams(vmem_limit_bytes=28 * 1024 * 1024),
        cost_estimate=pl.CostEstimate(flops=0, bytes_accessed=0, transcendentals=0),
        input_output_aliases=aliases or {},
        name=name,
    )


def body(frames, link_to_wire, neighbours, kernel, wide_filter, tight_filter, roi_mask):
    frames, roi_mask = frames[0], roi_mask[0]
    share, ticks = frames.shape
    blocks = lax.axis_size("chan")
    detectors = lax.axis_size("apa")
    padded = max(kernel.shape[1], lane // 2)
    width = 2 * padded
    wires = link_to_wire if share % lane == 0 else link_to_wire.reshape(blocks, share)
    table = jnp.asarray(forward_tables(ticks, blocks, padded))

    def around(parts):
        return [
            near(lax.ppermute(part, "chan", [(i, (i + s) % blocks) for i in range(blocks)]))
            for s, part in enumerate(parts, 1)
        ]

    first = call(
        functools.partial(tick_spectra, blocks),
        [((share, width), bf16)] * (blocks - 1) + [((blocks * HALO_CH, width), bf16)] * 2
        + [((share, ticks), bf16), ((blocks, ticks, width), bf16), (wires.shape, jnp.int32), (neighbours.shape, jnp.int32)],
        [pinned] * 4, "tick_spectra", [pltpu.SemaphoreType.DMA((7,))],
    )(*map(distant, (frames, table, wires, neighbours)))
    far, bands = first[: blocks - 1], first[blocks - 1 : blocks + 1]
    frames, table, wires, neighbours = map(near, first[blocks + 1 :])
    received = around(far)
    tables = [channel_tables(planes[i].length, planes[i].rows, order) for i, order in ((0, (0, 1, 0)), (2, (0, 1)))]
    sources = [kernel, *map(jnp.asarray, tables)]
    folded, *ready = call(
        lambda *refs: near_part(refs[:3], *refs[3:]),
        [((all_rows, 2 * width), f32)] + [(part.shape, part.dtype) for part in sources],
        [pinned] * 3 + [whole] * 3, "near_part", [pltpu.SemaphoreType.DMA((3,))],
    )(*map(distant, sources), wires, frames, table)
    halo = []
    for step, band in zip((1, -1), bands):
        pairs = [(a, a + step) for a in range(detectors) if 0 <= a + step < detectors]
        halo.append(lax.ppermute(band, "apa", pairs))
    *halo, folded = lax.optimization_barrier((*halo, folded))
    shares = [
        jnp.concatenate([band[s * HALO_CH : (s + 1) * HALO_CH] for band in halo]) for s in range(1, blocks)
    ]
    halo = [near(band) for band in halo] + around(shares)
    kernel, narrow, wide = map(near, ready)
    folded = near(folded)
    sums, diffs = map(near, call(
        kernel_factors, [((all_rows, 2 * width), f32)] * 2, [whole], "kernel_factors",
    )(kernel))
    basis = jnp.asarray(inverse_tables(ticks, blocks, padded))
    filters = (wide_filter[None], tight_filter[None])
    mask = jnp.transpose(roi_mask)
    signal_shapes = [
        ((share, ticks), f32), ((max(blocks - 1, 1), 2 * width, 2 * ticks), bf16), ((share, ticks), f32)
    ]

    def own_part(own):
        return map(near, call(
            functools.partial(own_signal, blocks), signal_shapes,
            [whole, pinned] + [whole] * 3, "own_signal",
            [pltpu.VMEM(basis.shape, f32), pltpu.SemaphoreType.DMA],
        )(near(own), distant(basis), *filters, mask))

    if blocks != 2:
        own, *sends = call(
            functools.partial(all_planes, blocks, share),
            [((share, width), f32)] + [((share, width), bf16)] * (blocks - 1),
            [whole] * (2 * blocks + 7), "all_planes",
            [pltpu.VMEM((CHANNELS, width), f32)],
        )(neighbours, *received, *halo, wires, folded, sums, diffs, narrow, wide)
        returned = around(sends)
        signal, bases, inside = own_part(own)
        out = pl.pallas_call(
            functools.partial(whole_signal, blocks),
            out_shape=jax.ShapeDtypeStruct((share, ticks), f32),
            in_specs=[whole] * (blocks + 2),
            out_specs=whole,
            name="whole_signal",
        )(signal, bases, inside, *returned)
        return out[None]

    more = share - PW
    sent, rest, *operands = call(
        functools.partial(leading_planes, share),
        [((PW, width), bf16), ((PU + PV - PW, width), f32), ((1, share), jnp.int32), ((share, 2 * width), bf16)],
        [whole] * 11, "leading_planes", [pltpu.VMEM((PU + PV, width), f32)],
    )(neighbours, *received, *halo, wires, folded, sums, diffs, narrow, wide)
    (early,) = around([sent])
    sent, own = call(
        functools.partial(trailing_planes, share), [((more, width), bf16), ((share, width), f32)],
        [whole] * 12, "trailing_planes", [pltpu.VMEM((PU + PV, width), f32)],
    )(neighbours, *halo, *map(near, operands), near(rest), folded, sums, diffs, narrow, wide)
    (late,) = around([sent])
    signal, bases, inside = own_part(own)

    def finish(values, spans, *before):
        step = math.gcd(PW, more) // 2
        rows = max(count for _, count in spans)
        (out,) = call(
            functools.partial(part_signal, spans), [((share, ticks), f32)],
            [whole] * 4 + [pinned] * len(before), "part_signal",
            [pltpu.VMEM((rows, ticks), f32), pltpu.SemaphoreType.DMA((rows // step,))],
            final=True, aliases={4: 0} if before else None,
        )(signal, bases, inside, values, *before)
        return out

    out = finish(early, ((0, PW), (more, PW)))
    return finish(late, ((PW, more), (0, more)), out)[None]


def solution(mesh):
    placed = (
        P("apa", "chan", None),
        P("apa", None),
        P("apa", None),
        P(None, "chan", None),
        P(),
        P(),
        P("apa", "chan", None),
    )
    return jax.shard_map(
        body, mesh=mesh, in_specs=placed, out_specs=P("apa", "chan", None), check_vma=False
    )
```

```python
import functools
import math

import jax
import jax.numpy as jnp
import ml_dtypes
import numpy as np
from jax import lax
from jax.experimental import pallas as pl
from jax.experimental.pallas import tpu as pltpu
from jax.sharding import PartitionSpec as P

PU = 800
PV = 800
PW = 960
HALO_CH = 128
BC = 16
BT = 64
CHANNELS = 2560

two_pi = 2.0 * math.pi
lane = 128
f32 = jnp.float32
bf16 = jnp.bfloat16
whole = pl.BlockSpec(memory_space=pltpu.VMEM)
pinned = pl.BlockSpec(memory_space=pltpu.HBM)


def near(array):
    return pltpu.with_memory_space_constraint(array, pltpu.VMEM)


def distant(array):
    return pltpu.with_memory_space_constraint(array, pltpu.HBM)


def ceil_to(size, step):
    return -(-size // step) * step


class Plane:
    def __init__(self, length, wire, count, keep, kernel_start, row):
        self.length, self.wire, self.count, self.keep = length, wire, count, keep
        self.kernel_start, self.row = kernel_start, row
        self.half = length // 2
        self.rows = ceil_to(self.half + 1, 16)


def make_planes():
    found, row, start = [], 0, 0
    for length, wire, count, keep in (
        (PU, 0, PU, 0),
        (PV, PU, PV, 0),
        (PW + 2 * HALO_CH, PU + PV, PW, HALO_CH),
    ):
        found.append(Plane(length, wire, count, keep, start, row))
        row += found[-1].rows
        start += length
    return found


planes = make_planes()
all_rows = planes[-1].row + planes[-1].rows


def split(values):
    high = values.astype(bf16)
    return high, (values - high.astype(f32)).astype(bf16)


def channel_tables(length, rows):
    index = np.arange(rows)
    angles = (index[:, None] * index[None, :] % length) * (two_pi / length)
    inside = (index <= length // 2).astype(np.float64)
    mask = inside[:, None] * inside[None, :]
    found = []
    for values in (np.cos(angles) * mask, np.sin(angles) * mask):
        high = values.astype(np.float32).astype(ml_dtypes.bfloat16)
        low = (values - high.astype(np.float64)).astype(np.float32).astype(ml_dtypes.bfloat16)
        found.append(np.concatenate([high, low], axis=1))
    return np.stack(found)


def tick_angles(ticks):
    return (np.arange(ticks)[:, None] * np.arange(ticks // 2)[None, :] % ticks) * (two_pi / ticks)


def in_blocks(values, blocks, padded):
    parts = np.stack(np.split(values, blocks, axis=-1))
    return np.pad(parts, [(0, 0)] * (parts.ndim - 1) + [(0, padded - parts.shape[-1])])


def forward_tables(ticks, blocks, padded):
    angles = tick_angles(ticks)
    halves = [in_blocks(part, blocks, padded) for part in (np.cos(angles), -np.sin(angles))]
    return np.concatenate(halves, axis=-1).astype(np.float32).astype(ml_dtypes.bfloat16)


def inverse_tables(ticks, blocks, padded):
    angles = tick_angles(ticks)
    weights = np.where(np.arange(ticks // 2) == 0, 1.0, 2.0) / ticks
    halves = [in_blocks(part * weights, blocks, padded) for part in (np.cos(angles), -np.sin(angles))]
    return np.ascontiguousarray(np.swapaxes(np.concatenate(halves, axis=-1), 1, 2)).astype(np.float32)


def dot(left, right):
    return jnp.dot(left, right, preferred_element_type=f32)


def one_hot(rows, first, targets):
    numbers = lax.broadcasted_iota(jnp.int16, (rows, targets.shape[1]), 0)
    return jnp.where(numbers == (targets - first).astype(jnp.int16), bf16(1), bf16(0))


def wires_of(wires, block, share):
    if wires.shape[0] > 1:
        return wires[pl.ds(block, 1), :]
    return wires[:, pl.ds(pl.multiple_of(block * share, lane), share)]


def tick_spectra(blocks, frames_source, table_source, wires_source, neighbours_source, *refs):
    outs, (frames, table, wires, neighbours, sems) = refs[: blocks - 1], refs[blocks - 1 :]
    parts = 4
    size = frames.shape[0] // parts
    spans = [pl.ds(i * size, size) for i in range(parts)]
    pairs = [(table_source, table)] + [(frames_source.at[span], frames.at[span]) for span in spans]
    pairs += [(wires_source, wires), (neighbours_source, neighbours)]
    copies = [pltpu.make_async_copy(source, target, sems.at[i]) for i, (source, target) in enumerate(pairs)]
    for copy in copies:
        copy.start()
    copies[0].wait()
    here = lax.axis_index("chan")
    for copy, span in zip(copies[1:], spans):
        copy.wait()
        for s, out in enumerate(outs, 1):
            out[span, :] = dot(frames[span, :], table[lax.rem(here + s, blocks)]).astype(bf16)
    for copy in copies[1 + parts :]:
        copy.wait()


def partners(detector):
    odd = detector % 2
    return detector + 1 - 2 * odd, detector - 1 + 2 * odd


def edge_bands(blocks, neighbours, frames, table, wires, *bands):
    here = lax.axis_index("chan")
    mine = wires_of(wires, here, frames.shape[0])
    for other, out in zip(partners(lax.axis_index("apa")), bands):
        first = jnp.where(neighbours[:, 1:2] == other, CHANNELS - HALO_CH, PU + PV)
        rows = dot(one_hot(HALO_CH, first, mine), frames[...]).astype(bf16)
        for s in range(blocks):
            spectra = dot(rows, table[lax.rem(here + s, blocks)])
            out[s * HALO_CH : (s + 1) * HALO_CH, :] = spectra.astype(bf16)


def lane_signs(width):
    return jnp.where(lax.broadcasted_iota(jnp.int32, (1, width), 1) < width // 2, 1.0, -1.0)


def rotated(values):
    width = values.shape[1]
    return pltpu.roll(values, width // 2, 1) * lane_signs(width)


def spread(values):
    width = values.shape[1]
    first = lax.broadcasted_iota(jnp.int32, values.shape, 1) < width // 2
    other = pltpu.roll(values, width // 2, 1)
    return jnp.concatenate([jnp.where(first, values, other), jnp.where(first, other, values)], axis=1)


def fold_of(offset, length, row):
    behind = 2 * offset > length
    return row + jnp.where(behind, length - offset, offset), jnp.where(behind, -1.0, 1.0)


def fold_of_wires(wires):
    first, second = wires < PU, wires < PU + PV
    offset = jnp.where(first, wires, jnp.where(second, wires - PU, wires - (PU + PV) + HALO_CH))
    length = jnp.where(first, PU, jnp.where(second, PV, planes[2].length))
    row = jnp.where(first, planes[0].row, jnp.where(second, planes[1].row, planes[2].row))
    return fold_of(offset, length, row)


def fold_of_halo(begin):
    offset = lax.broadcasted_iota(jnp.int32, (1, HALO_CH), 1) + begin
    return fold_of(offset, planes[2].length, planes[2].row)


def sign_columns(signs, width):
    return jnp.transpose(jnp.broadcast_to(signs, (width, signs.shape[1]))) * lane_signs(width)


def backwards(count, last, limit, product):
    parts = []
    for start in range(0, count, lane):
        size = min(lane, count - start)
        high, low = min(last - start, limit - 1), max(last - start - size + 1, 0)
        first = low // lane * lane
        stop = min(ceil_to(high + 1, lane), limit)
        row = lax.broadcasted_iota(jnp.int32, (size, stop - first), 0)
        column = lax.broadcasted_iota(jnp.int32, (size, stop - first), 1)
        matrix = jnp.where(column == last - start - first - row, 1.0, 0.0).astype(bf16)
        parts.append(product(matrix, first, stop))
    return jnp.concatenate(parts, axis=0)


def fold_operand(spectra, signs):
    width = spectra.shape[1]
    turned = pltpu.roll(spectra.astype(f32), width // 2, 1) * signs
    return jnp.concatenate([spectra, turned.astype(bf16)], axis=1)


def near_part(sources, wires, frames, table, folded, *refs):
    kept, sems = refs[:-1], refs[-1]
    copies = [pltpu.make_async_copy(source, target, sems.at[i]) for i, (source, target) in enumerate(zip(sources, kept))]
    for copy in copies:
        copy.start()
    here = lax.axis_index("chan")
    width = folded.shape[1] // 2
    targets, signs = fold_of_wires(wires_of(wires, here, frames.shape[0]))
    spectra = dot(frames[...], table[here])
    turned = pltpu.roll(spectra, width // 2, 1) * sign_columns(signs, width)
    operand = jnp.concatenate(split(spectra) + split(turned), axis=1)
    for plane in planes:
        rows = pl.ds(plane.row, plane.rows)
        both = dot(one_hot(plane.rows, plane.row, targets), operand)
        folded[rows, :width] = both[:, :width] + both[:, width : 2 * width]
        folded[rows, width:] = both[:, 2 * width : 3 * width] + both[:, 3 * width :]
    for copy in copies:
        copy.wait()


def factors(blocks, share, kernel, wires, sums, diffs, chosen, far_signs):
    harmonics, width = kernel.shape[1], sums.shape[1] // 2
    spare = width // 2 - harmonics
    for plane in planes:
        rows = pl.ds(plane.row, plane.rows)
        start = plane.kernel_start // lane * lane
        stop = ceil_to(plane.kernel_start + plane.length, lane)
        offset = plane.kernel_start - start
        parts = []
        for z in range(2):
            parts.append(kernel[z, :, start:stop])
            if spare:
                parts.append(jnp.zeros((spare, stop - start), f32))
        values = jnp.concatenate(parts, axis=0)
        direct = jnp.transpose(values[:, : ceil_to(offset + plane.rows, lane)])[offset : offset + plane.rows]
        pair = jnp.concatenate(split(values), axis=0)

        def product(matrix, first, stop):
            return lax.dot_general(
                matrix, pair[:, first:stop], (((1,), (1,)), ((), ())), preferred_element_type=f32
            )

        both = backwards(plane.rows, plane.length + offset, stop - start, product)
        mirror = (both[:, :width] + both[:, width:]) * (1.0 / plane.length)
        row = lax.broadcasted_iota(jnp.int32, (plane.rows, width), 0)
        direct = jnp.where(row <= plane.half, direct * (1.0 / plane.length), 0.0)
        mirror = jnp.where((row > 0) & (row < plane.half), mirror, 0.0)
        sums[rows, :] = spread(direct + mirror)
        diffs[rows, :] = spread(direct - mirror)
    here = lax.axis_index("chan")
    for s in range(1, blocks):
        targets, signs = fold_of_wires(wires_of(wires, lax.rem(here + blocks - s, blocks), share))
        span = pl.ds((s - 1) * share, share)
        chosen[:, span] = one_hot(all_rows, 0, targets)
        far_signs[span, :] = sign_columns(signs, width)


def multiplied(even, odd, plus, minus):
    width = even.shape[1]
    even_turned, odd_turned = rotated(even), rotated(odd)
    plus_re, plus_im, minus_re, minus_im = plus[:, :width], plus[:, width:], minus[:, :width], minus[:, width:]
    total = (even * plus_re + odd * minus_re) - (even_turned * plus_im + odd_turned * minus_im)
    gap = (even * minus_im + odd * plus_im) + (even_turned * minus_re + odd_turned * plus_re)
    return total, -gap


def halo_operand(blocks, neighbours, halo):
    bands, targets, signs = [], [], []
    lower, upper = neighbours[:, 0:1], neighbours[:, 1:2]
    never = -4 * planes[2].length
    for way, other in enumerate(partners(lax.axis_index("apa"))):
        total = halo[way][:HALO_CH, :].astype(f32)
        for ref in halo[2:]:
            total += ref[way * HALO_CH : (way + 1) * HALO_CH, :].astype(f32)
        bands.append(total.astype(bf16))
        begin = jnp.where(upper == other, planes[2].length - HALO_CH, never)
        begin = jnp.where(lower == other, 0, begin)
        target, sign = fold_of_halo(jnp.where(other < 0, never, begin))
        targets.append(target)
        signs.append(sign)
    signs = sign_columns(jnp.concatenate(signs, axis=1), bands[0].shape[1])
    operand = fold_operand(jnp.concatenate(bands, axis=0), signs)
    return jnp.concatenate(targets, axis=1), operand


def transform(table, values):
    width = values.shape[1]
    joined = jnp.concatenate(split(values), axis=1)
    result = dot(table, jnp.concatenate([joined, joined], axis=0))
    return result[:, :width] + result[:, width:]


def to_frequencies(plane, chosen, operand, bands, folded, sums, diffs, table):
    rows = pl.ds(plane.row, plane.rows)
    both = folded[rows, :] + dot(chosen[rows, :], operand)
    if bands is not None:
        both += dot(one_hot(plane.rows, plane.row, bands[0]), bands[1])
    width = both.shape[1] // 2
    even, odd = transform(table[0], both[:, :width]), transform(table[1], both[:, width:])
    return multiplied(even, odd, sums[rows, :], diffs[rows, :])


def to_channels(result, plane, total, gap, table):
    cosine, sine = transform(table[0, plane.keep :], total), transform(table[1, plane.keep :], gap)
    straight, width = plane.count // 2, total.shape[1]
    result[:straight, :] = (cosine + sine)[:straight]
    back = jnp.concatenate(split(cosine - sine), axis=1)
    turned = backwards(
        straight, plane.half - plane.keep, back.shape[0], lambda matrix, first, stop: dot(matrix, back[first:stop])
    )
    result[straight : plane.count, :] = turned[:, :width] + turned[:, width:]


def put(result, plane, chosen, operand, bands, folded, sums, diffs, table):
    total, gap = to_frequencies(plane, chosen, operand, bands, folded, sums, diffs, table)
    to_channels(result, plane, total, gap, table)


def all_planes(blocks, share, neighbours, *refs):
    received, halo = refs[: blocks - 1], refs[blocks - 1 : 2 * blocks]
    chosen, far_signs, folded, sums, diffs, narrow, wide, own = refs[2 * blocks : 2 * blocks + 8]
    sends, result = refs[2 * blocks + 8 : 3 * blocks + 7], refs[3 * blocks + 7]
    operand = fold_operand(jnp.concatenate([ref[...] for ref in received], axis=0), far_signs[...])
    for plane in planes:
        bands = halo_operand(blocks, neighbours, halo) if plane.keep else None
        operands = (chosen, operand, bands, folded, sums, diffs, wide if plane.keep else narrow)
        put(result.at[pl.ds(plane.wire, plane.count)], plane, *operands)
    here = lax.axis_index("chan")
    own[...] = result[pl.ds(pl.multiple_of(here * share, share), share), :]
    for shift, out in enumerate(sends, 1):
        first = pl.multiple_of(lax.rem(here + shift, blocks) * share, share)
        out[...] = result[pl.ds(first, share), :].astype(bf16)


def middle_plane(share, far, chosen, far_signs, folded, sums, diffs, narrow, wide_source, send, own, operand, wide, result, sem):
    copy = pltpu.make_async_copy(wide_source, wide, sem)
    copy.start()
    middle = planes[1]
    operand[...] = fold_operand(far[...], far_signs[...])
    put(result, middle, chosen, operand[...], None, folded, sums, diffs, narrow)
    below = share - middle.wire
    above = middle.count - below

    @pl.when(lax.axis_index("chan") == 0)
    def _():
        send[:above, :] = result[below:, :].astype(bf16)
        send[above:, :] = jnp.zeros((below - above, send.shape[1]), bf16)
        own[...] = result[:below, :]

    @pl.when(lax.axis_index("chan") != 0)
    def _():
        send[...] = result[:below, :].astype(bf16)
        own[:above, :] = result[below:, :]
        own[above:, :] = jnp.zeros((below - above, own.shape[1]), f32)

    copy.wait()


def outer_plane(neighbours, halo0, halo1, halo2, operand, chosen, folded, sums, diffs, narrow, wide, send, total, gap, result):
    first, _, last = planes
    bands = halo_operand(2, neighbours, (halo0, halo1, halo2))

    @pl.when(lax.axis_index("chan") == 0)
    def _():
        put(result, last, chosen, operand[...], bands, folded, sums, diffs, wide)
        send[...] = result[...].astype(bf16)

    @pl.when(lax.axis_index("chan") != 0)
    def _():
        put(result, first, chosen, operand[...], None, folded, sums, diffs, narrow)
        send[: first.count, :] = result[: first.count, :].astype(bf16)
        send[first.count :, :] = jnp.zeros((last.count - first.count, send.shape[1]), bf16)
        total[...], gap[...] = to_frequencies(last, chosen, operand[...], bands, folded, sums, diffs, wide)


def inner_plane(operand, chosen, folded, sums, diffs, narrow, wide, total, gap, part, own):
    first, middle, last = planes
    above = own.shape[0] - last.count

    @pl.when(lax.axis_index("chan") == 0)
    def _():
        put(own, first, chosen, operand[...], None, folded, sums, diffs, narrow)
        own[first.count :, :] = part[...]

    @pl.when(lax.axis_index("chan") != 0)
    def _():
        to_channels(own.at[pl.ds(above, last.count)], last, total[...], gap[...], wide)
        own[:above, :] = part[:above, :]


def spread_mask(mask, share, ticks):
    marked = jnp.where(mask == 1, 1.0, 0.0).astype(bf16)
    row = lax.broadcasted_iota(jnp.int32, (share, mask.shape[1]), 0)
    column = lax.broadcasted_iota(jnp.int32, (share, mask.shape[1]), 1)
    taken = jnp.where(row // BC == column, 1.0, 0.0).astype(bf16)
    rows = lax.dot_general(taken, marked, (((1,), (1,)), ((), ())), preferred_element_type=f32).astype(bf16)
    row = lax.broadcasted_iota(jnp.int32, (mask.shape[0], ticks), 0)
    column = lax.broadcasted_iota(jnp.int32, (mask.shape[0], ticks), 1)
    return dot(rows, jnp.where(column // BT == row, 1.0, 0.0).astype(bf16))


def chosen_signal(both, inside):
    ticks = inside.shape[1]
    return jnp.where(inside > 0.5, both[:, :ticks], both[:, ticks:])


def scaled_basis(block, blocks, basis, filters, harmonics):
    padded = basis.shape[1] // 2
    ticks = basis.shape[2]
    gains = []
    for gain in filters:
        columns = gain[...] if blocks == 1 else None
        for b in range(blocks):
            piece = gain[:, b * harmonics : (b + 1) * harmonics]
            columns = piece if columns is None else jnp.where(block == b, piece, columns)
        if padded > harmonics:
            columns = jnp.concatenate([columns, jnp.zeros((1, padded - harmonics), f32)], axis=1)
        columns = jnp.concatenate([columns, columns], axis=1)
        tall = jnp.transpose(jnp.broadcast_to(columns, (lane, 2 * padded)))
        gains.append(jnp.concatenate([tall] * (ticks // lane), axis=1))
    values = basis[block]
    return split(jnp.concatenate([values * part for part in gains], axis=1))


def own_signal(blocks, own, basis_source, wide_filter, tight_filter, mask, signal, bases, inside, basis, sem):
    basis_copy = pltpu.make_async_copy(basis_source, basis, sem)
    basis_copy.start()
    inside[...] = spread_mask(mask[...], own.shape[0], signal.shape[1])
    basis_copy.wait()
    here = lax.axis_index("chan")
    ticks = signal.shape[1]
    harmonics = wide_filter.shape[1] // blocks
    filters = (wide_filter, tight_filter)
    high, low = scaled_basis(here, blocks, basis, filters, harmonics)
    joined = jnp.concatenate(split(own[...]), axis=1)
    both = dot(joined, jnp.concatenate([high, high], axis=0))
    both += dot(joined, jnp.concatenate([low, low], axis=0))
    signal[...] = chosen_signal(both, inside[...])
    for shift in range(1, blocks):
        parts = scaled_basis(lax.rem(here + blocks - shift, blocks), blocks, basis, filters, harmonics)
        bases[shift - 1] = jnp.concatenate(parts, axis=0)


def whole_signal(blocks, signal, bases, inside, *refs):
    out = refs[-1]
    both = None
    for shift in range(1, blocks):
        values = refs[shift - 1][...]
        term = dot(jnp.concatenate([values, values], axis=1), bases[shift - 1])
        both = term if both is None else both + term
    if both is None:
        out[...] = signal[...]
    else:
        out[...] = signal[...] + chosen_signal(both, inside[...])


def part_signal(spans, signal, bases, inside, values, *refs):
    out, room, sems = refs[-3:]
    step = room.shape[0] // sems.shape[0]
    for device, (first, count) in enumerate(spans):

        @pl.when(lax.axis_index("chan") == device)
        def _(first=first, count=count):
            copies = []
            for i in range(count // step):
                some = values[i * step : (i + 1) * step, :]
                both = dot(jnp.concatenate([some, some], axis=1), bases[0])
                rows, slot = pl.ds(first + i * step, step), pl.ds(i * step, step)
                room[slot, :] = signal[rows, :] + chosen_signal(both, inside[rows, :])
                copies.append(pltpu.make_async_copy(room.at[slot], out.at[rows], sems.at[i]))
                copies[-1].start()
            for copy in copies:
                copy.wait()


costs = {
    "tick_spectra": 500, "edge_bands": 200, "near_part": 600, "factors": 575, "middle_plane": 650, "outer_plane": 1100,
    "inner_plane": 875, "own_signal": 500, "part_signal": 250, "all_planes": 2000,
}
costs = {name: cost * 1250000 for name, cost in costs.items()}


def call(kernel, outs, ins, name, scratch=(), final=False, aliases=None):
    kind = jax.ShapeDtypeStruct if final else pltpu.VMEM
    return pl.pallas_call(
        kernel,
        out_shape=[kind(shape, dtype) for shape, dtype in outs],
        in_specs=ins,
        out_specs=[pinned if final else whole] * len(outs),
        scratch_shapes=scratch,
        compiler_params=pltpu.CompilerParams(vmem_limit_bytes=28 * 1024 * 1024),
        cost_estimate=pl.CostEstimate(flops=costs[name], bytes_accessed=0, transcendentals=0),
        input_output_aliases=aliases or {},
        name=name,
    )


def body(frames, link_to_wire, neighbours, kernel, wide_filter, tight_filter, roi_mask):
    frames, roi_mask = frames[0], roi_mask[0]
    share, ticks = frames.shape
    blocks = lax.axis_size("chan")
    detectors = lax.axis_size("apa")
    padded = max(kernel.shape[1], lane // 2)
    width = 2 * padded
    wires = link_to_wire if share % lane == 0 else link_to_wire.reshape(blocks, share)
    table = jnp.asarray(forward_tables(ticks, blocks, padded))

    def around(parts):
        return [
            lax.ppermute(part, "chan", [(i, (i + s) % blocks) for i in range(blocks)])
            for s, part in enumerate(parts, 1)
        ]

    first = call(
        functools.partial(tick_spectra, blocks),
        [((share, width), bf16)] * (blocks - 1)
        + [((share, ticks), bf16), ((blocks, ticks, width), bf16), (wires.shape, jnp.int32), (neighbours.shape, jnp.int32)],
        [pinned] * 4, "tick_spectra", [pltpu.SemaphoreType.DMA((7,))],
    )(*map(distant, (frames, table, wires, neighbours)))
    frames, table, wires, neighbours = map(near, first[blocks - 1 :])
    received = list(map(near, around(first[: blocks - 1])))
    bands = call(
        functools.partial(edge_bands, blocks), [((blocks * HALO_CH, width), bf16)] * 2, [whole] * 4, "edge_bands",
    )(neighbours, frames, table, wires)
    narrow, wide = (jnp.asarray(channel_tables(planes[i].length, planes[i].rows)) for i in (0, 2))
    sources = [kernel, narrow] + ([wide] if blocks != 2 else [])
    folded, *ready = call(
        lambda *refs: near_part(refs[: len(sources)], *refs[len(sources) :]),
        [((all_rows, 2 * width), f32)] + [(part.shape, part.dtype) for part in sources],
        [pinned] * len(sources) + [whole] * 3, "near_part", [pltpu.SemaphoreType.DMA((len(sources),))],
    )(*map(distant, sources), wires, frames, table)
    halo = []
    for way, band in enumerate(bands):
        pairs = [(a, partners(a)[way]) for a in range(detectors) if 0 <= partners(a)[way] < detectors]
        halo.append(lax.ppermute(band, "apa", pairs))
    *halo, folded = lax.optimization_barrier((*halo, folded))
    shares = [
        jnp.concatenate([band[s * HALO_CH : (s + 1) * HALO_CH] for band in halo]) for s in range(1, blocks)
    ]
    halo = [near(band) for band in halo + around(shares)]
    kernel, narrow, *rest = map(near, ready)
    folded = near(folded)
    sums, diffs, chosen, far_signs = map(near, call(
        functools.partial(factors, blocks, share),
        [((all_rows, 2 * width), f32)] * 2 + [((all_rows, (blocks - 1) * share), bf16), (((blocks - 1) * share, width), f32)],
        [whole] * 2, "factors",
    )(kernel, wires))
    basis = jnp.asarray(inverse_tables(ticks, blocks, padded))
    filters = (wide_filter[None], tight_filter[None])
    mask = jnp.transpose(roi_mask)
    signal_shapes = [
        ((share, ticks), f32), ((max(blocks - 1, 1), 2 * width, 2 * ticks), bf16), ((share, ticks), f32)
    ]

    def own_part(own):
        return map(near, call(
            functools.partial(own_signal, blocks), signal_shapes,
            [whole, pinned] + [whole] * 3, "own_signal",
            [pltpu.VMEM(basis.shape, f32), pltpu.SemaphoreType.DMA],
        )(near(own), distant(basis), *filters, mask))

    if blocks != 2:
        own, *sends = call(
            functools.partial(all_planes, blocks, share),
            [((share, width), f32)] + [((share, width), bf16)] * (blocks - 1),
            [whole] * (2 * blocks + 8), "all_planes",
            [pltpu.VMEM((CHANNELS, width), f32)],
        )(neighbours, *received, *halo, chosen, far_signs, folded, sums, diffs, narrow, *rest)
        returned = map(near, around(sends))
        signal, bases, inside = own_part(own)
        out = pl.pallas_call(
            functools.partial(whole_signal, blocks),
            out_shape=jax.ShapeDtypeStruct((share, ticks), f32),
            in_specs=[whole] * (blocks + 2),
            out_specs=whole,
            name="whole_signal",
        )(signal, bases, inside, *returned)
        return out[None]

    below, above = share - PU, share - PW
    sent, part, operand, wide = call(
        functools.partial(middle_plane, share),
        [((below, width), bf16), ((below, width), f32), ((share, 2 * width), bf16), (wide.shape, bf16)],
        [whole] * 7 + [pinned], "middle_plane", [pltpu.VMEM((PV, width), f32), pltpu.SemaphoreType.DMA],
    )(*received, chosen, far_signs, folded, sums, diffs, narrow, distant(wide))
    (early,) = around([sent])
    operands = (near(operand), chosen, folded, sums, diffs, narrow, near(wide))
    last = ((planes[2].rows, width), f32)
    sent, total, gap = call(
        outer_plane, [((PW, width), bf16), last, last], [whole] * 11, "outer_plane", [pltpu.VMEM((PW, width), f32)],
    )(neighbours, *halo, *operands)
    sent, early = lax.optimization_barrier((sent, early))
    (late,) = map(near, around([sent]))
    (own,) = call(inner_plane, [((share, width), f32)], [whole] * 10, "inner_plane")(*operands, *map(near, (total, gap, part)))
    signal, bases, inside = own_part(own)

    def finish(values, spans, *before):
        step = math.gcd(PU, PW)
        rows = max(count for _, count in spans)
        (out,) = call(
            functools.partial(part_signal, spans), [((share, ticks), f32)],
            [whole] * 4 + [pinned] * len(before), "part_signal",
            [pltpu.VMEM((rows, ticks), f32), pltpu.SemaphoreType.DMA((rows // step,))],
            final=True, aliases={4: 0} if before else None,
        )(signal, bases, inside, values, *before)
        return out

    out = finish(near(early), ((PU, below), (0, above)))
    return finish(late, ((0, PU), (above, PW)), out)[None]


def solution(mesh):
    placed = (
        P("apa", "chan", None),
        P("apa", None),
        P("apa", None),
        P(None, "chan", None),
        P(),
        P(),
        P("apa", "chan", None),
    )
    return jax.shard_map(
        body, mesh=mesh, in_specs=placed, out_specs=P("apa", "chan", None), check_vma=False
    )
```

```python
import functools
import math

import jax
import jax.numpy as jnp
import ml_dtypes
import numpy as np
from jax import lax
from jax.experimental import pallas as pl
from jax.experimental.pallas import tpu as pltpu
from jax.sharding import PartitionSpec as P

PU = 800
PV = 800
PW = 960
HALO_CH = 128
BC = 16
BT = 64
CHANNELS = 2560

two_pi = 2.0 * math.pi
lane = 128
f32 = jnp.float32
bf16 = jnp.bfloat16
whole = pl.BlockSpec(memory_space=pltpu.VMEM)
pinned = pl.BlockSpec(memory_space=pltpu.HBM)


def near(array):
    return pltpu.with_memory_space_constraint(array, pltpu.VMEM)


def distant(array):
    return pltpu.with_memory_space_constraint(array, pltpu.HBM)


def ceil_to(size, step):
    return -(-size // step) * step


class Plane:
    def __init__(self, length, wire, count, keep, kernel_start, row):
        self.length, self.wire, self.count, self.keep = length, wire, count, keep
        self.kernel_start, self.row = kernel_start, row
        self.half = length // 2
        self.rows = ceil_to(self.half + 1, 16)


def make_planes():
    found, row, start = [], 0, 0
    for length, wire, count, keep in (
        (PU, 0, PU, 0),
        (PV, PU, PV, 0),
        (PW + 2 * HALO_CH, PU + PV, PW, HALO_CH),
    ):
        found.append(Plane(length, wire, count, keep, start, row))
        row += found[-1].rows
        start += length
    return found


planes = make_planes()
all_rows = planes[-1].row + planes[-1].rows


def split(values):
    high = values.astype(bf16)
    return high, (values - high.astype(f32)).astype(bf16)


def channel_tables(length, rows, order):
    index = np.arange(rows)
    angles = (index[:, None] * index[None, :] % length) * (two_pi / length)
    inside = (index <= length // 2).astype(np.float64)
    mask = inside[:, None] * inside[None, :]
    found = []
    for values in (np.cos(angles) * mask, np.sin(angles) * mask):
        high = values.astype(np.float32).astype(ml_dtypes.bfloat16)
        low = (values - high.astype(np.float64)).astype(np.float32).astype(ml_dtypes.bfloat16)
        found.append(np.concatenate([(high, low)[i] for i in order], axis=1))
    return np.stack(found)


def tick_angles(ticks):
    return (np.arange(ticks)[:, None] * np.arange(ticks // 2)[None, :] % ticks) * (two_pi / ticks)


def in_blocks(values, blocks, padded):
    parts = np.stack(np.split(values, blocks, axis=-1))
    return np.pad(parts, [(0, 0)] * (parts.ndim - 1) + [(0, padded - parts.shape[-1])])


def forward_tables(ticks, blocks, padded):
    angles = tick_angles(ticks)
    halves = [in_blocks(part, blocks, padded) for part in (np.cos(angles), -np.sin(angles))]
    return np.concatenate(halves, axis=-1).astype(np.float32).astype(ml_dtypes.bfloat16)


def inverse_tables(ticks, blocks, padded):
    angles = tick_angles(ticks)
    weights = np.where(np.arange(ticks // 2) == 0, 1.0, 2.0) / ticks
    halves = [in_blocks(part * weights, blocks, padded) for part in (np.cos(angles), -np.sin(angles))]
    return np.ascontiguousarray(np.swapaxes(np.concatenate(halves, axis=-1), 1, 2)).astype(np.float32)


def dot(left, right):
    return jnp.dot(left, right, preferred_element_type=f32)


def one_hot(rows, first, targets):
    numbers = lax.broadcasted_iota(jnp.int16, (rows, targets.shape[1]), 0)
    return jnp.where(numbers == (targets - first).astype(jnp.int16), bf16(1), bf16(0))


def wires_of(wires, block, share):
    if wires.shape[0] > 1:
        return wires[pl.ds(block, 1), :]
    return wires[:, pl.ds(pl.multiple_of(block * share, lane), share)]


def tick_spectra(blocks, frames_source, table_source, wires_source, neighbours_source, *refs):
    outs, (frames, table, wires, neighbours, sems) = refs[: blocks - 1], refs[blocks - 1 :]
    parts = 4
    size = frames.shape[0] // parts
    spans = [pl.ds(i * size, size) for i in range(parts)]
    pairs = [(table_source, table)] + [(frames_source.at[span], frames.at[span]) for span in spans]
    pairs += [(wires_source, wires), (neighbours_source, neighbours)]
    copies = [pltpu.make_async_copy(source, target, sems.at[i]) for i, (source, target) in enumerate(pairs)]
    for copy in copies:
        copy.start()
    copies[0].wait()
    here = lax.axis_index("chan")
    for copy, span in zip(copies[1:], spans):
        copy.wait()
        for s, out in enumerate(outs, 1):
            out[span, :] = dot(frames[span, :], table[lax.rem(here + s, blocks)]).astype(bf16)
    for copy in copies[1 + parts :]:
        copy.wait()


def partners(detector):
    odd = detector % 2
    return detector + 1 - 2 * odd, detector - 1 + 2 * odd


def edge_bands(blocks, neighbours, frames, table, wires, *bands):
    here = lax.axis_index("chan")
    mine = wires_of(wires, here, frames.shape[0])
    for other, out in zip(partners(lax.axis_index("apa")), bands):
        first = jnp.where(neighbours[:, 1:2] == other, CHANNELS - HALO_CH, PU + PV)
        rows = dot(one_hot(HALO_CH, first, mine), frames[...]).astype(bf16)
        for s in range(blocks):
            spectra = dot(rows, table[lax.rem(here + s, blocks)])
            out[s * HALO_CH : (s + 1) * HALO_CH, :] = spectra.astype(bf16)


def lane_signs(width):
    return jnp.where(lax.broadcasted_iota(jnp.int32, (1, width), 1) < width // 2, 1.0, -1.0)


def rotated(values):
    width = values.shape[1]
    return pltpu.roll(values, width // 2, 1) * lane_signs(width)


def spread(values):
    width = values.shape[1]
    first = lax.broadcasted_iota(jnp.int32, values.shape, 1) < width // 2
    other = pltpu.roll(values, width // 2, 1)
    return jnp.concatenate([jnp.where(first, values, other), jnp.where(first, other, values)], axis=1)


def fold_of(offset, length, row):
    behind = 2 * offset > length
    return row + jnp.where(behind, length - offset, offset), jnp.where(behind, -1.0, 1.0)


def fold_of_wires(wires):
    first, second = wires < PU, wires < PU + PV
    offset = jnp.where(first, wires, jnp.where(second, wires - PU, wires - (PU + PV) + HALO_CH))
    length = jnp.where(first, PU, jnp.where(second, PV, planes[2].length))
    row = jnp.where(first, planes[0].row, jnp.where(second, planes[1].row, planes[2].row))
    return fold_of(offset, length, row)


def fold_of_halo(begin):
    offset = lax.broadcasted_iota(jnp.int32, (1, HALO_CH), 1) + begin
    return fold_of(offset, planes[2].length, planes[2].row)


def sign_columns(signs, width):
    return jnp.transpose(jnp.broadcast_to(signs, (width, signs.shape[1]))) * lane_signs(width)


def backwards(count, last, limit, product):
    parts = []
    for start in range(0, count, lane):
        size = min(lane, count - start)
        high, low = min(last - start, limit - 1), max(last - start - size + 1, 0)
        first = low // lane * lane
        stop = min(ceil_to(high + 1, lane), limit)
        row = lax.broadcasted_iota(jnp.int32, (size, stop - first), 0)
        column = lax.broadcasted_iota(jnp.int32, (size, stop - first), 1)
        matrix = jnp.where(column == last - start - first - row, 1.0, 0.0).astype(bf16)
        parts.append(product(matrix, first, stop))
    return jnp.concatenate(parts, axis=0)


def fold_operand(spectra, signs):
    width = spectra.shape[1]
    turned = pltpu.roll(spectra.astype(f32), width // 2, 1) * signs
    return jnp.concatenate([spectra, turned.astype(bf16)], axis=1)


def near_part(sources, wires, frames, table, folded, *refs):
    kept, sems = refs[:-1], refs[-1]
    copies = [pltpu.make_async_copy(source, target, sems.at[i]) for i, (source, target) in enumerate(zip(sources, kept))]
    for copy in copies:
        copy.start()
    here = lax.axis_index("chan")
    width = folded.shape[1] // 2
    targets, signs = fold_of_wires(wires_of(wires, here, frames.shape[0]))
    spectra = dot(frames[...], table[here])
    turned = pltpu.roll(spectra, width // 2, 1) * sign_columns(signs, width)
    operand = jnp.concatenate(split(spectra) + split(turned), axis=1)
    for plane in planes:
        rows = pl.ds(plane.row, plane.rows)
        both = dot(one_hot(plane.rows, plane.row, targets), operand)
        folded[rows, :width] = both[:, :width] + both[:, width : 2 * width]
        folded[rows, width:] = both[:, 2 * width : 3 * width] + both[:, 3 * width :]
    for copy in copies:
        copy.wait()


def factors(blocks, share, kernel, wires, wide_source, sums, diffs, chosen, far_signs, wide, sem):
    copy = pltpu.make_async_copy(wide_source, wide, sem)
    copy.start()
    harmonics, width = kernel.shape[1], sums.shape[1] // 2
    spare = width // 2 - harmonics
    for plane in planes:
        rows = pl.ds(plane.row, plane.rows)
        start = plane.kernel_start // lane * lane
        stop = ceil_to(plane.kernel_start + plane.length, lane)
        offset = plane.kernel_start - start
        parts = []
        for z in range(2):
            parts.append(kernel[z, :, start:stop])
            if spare:
                parts.append(jnp.zeros((spare, stop - start), f32))
        values = jnp.concatenate(parts, axis=0)
        direct = jnp.transpose(values[:, : ceil_to(offset + plane.rows, lane)])[offset : offset + plane.rows]
        pair = jnp.concatenate(split(values), axis=0)

        def product(matrix, first, stop):
            return lax.dot_general(
                matrix, pair[:, first:stop], (((1,), (1,)), ((), ())), preferred_element_type=f32
            )

        both = backwards(plane.rows, plane.length + offset, stop - start, product)
        mirror = (both[:, :width] + both[:, width:]) * (1.0 / plane.length)
        row = lax.broadcasted_iota(jnp.int32, (plane.rows, width), 0)
        direct = jnp.where(row <= plane.half, direct * (1.0 / plane.length), 0.0)
        mirror = jnp.where((row > 0) & (row < plane.half), mirror, 0.0)
        sums[rows, :] = spread(direct + mirror)
        diffs[rows, :] = spread(direct - mirror)
    here = lax.axis_index("chan")
    for s in range(1, blocks):
        targets, signs = fold_of_wires(wires_of(wires, lax.rem(here + blocks - s, blocks), share))
        span = pl.ds((s - 1) * share, share)
        chosen[:, span] = one_hot(all_rows, 0, targets)
        far_signs[span, :] = sign_columns(signs, width)
    copy.wait()


def multiplied(even, odd, plus, minus):
    width = even.shape[1]
    even_turned, odd_turned = rotated(even), rotated(odd)
    plus_re, plus_im, minus_re, minus_im = plus[:, :width], plus[:, width:], minus[:, :width], minus[:, width:]
    total = (even * plus_re + odd * minus_re) - (even_turned * plus_im + odd_turned * minus_im)
    gap = (even * minus_im + odd * plus_im) + (even_turned * minus_re + odd_turned * plus_re)
    return total, -gap


def halo_operand(blocks, neighbours, halo):
    bands, targets, signs = [], [], []
    lower, upper = neighbours[:, 0:1], neighbours[:, 1:2]
    never = -4 * planes[2].length
    for way, other in enumerate(partners(lax.axis_index("apa"))):
        total = halo[way][:HALO_CH, :].astype(f32)
        for ref in halo[2:]:
            total += ref[way * HALO_CH : (way + 1) * HALO_CH, :].astype(f32)
        bands.append(total.astype(bf16))
        begin = jnp.where(upper == other, planes[2].length - HALO_CH, never)
        begin = jnp.where(lower == other, 0, begin)
        target, sign = fold_of_halo(jnp.where(other < 0, never, begin))
        targets.append(target)
        signs.append(sign)
    signs = sign_columns(jnp.concatenate(signs, axis=1), bands[0].shape[1])
    operand = fold_operand(jnp.concatenate(bands, axis=0), signs)
    return jnp.concatenate(targets, axis=1), operand


def one_plane(table, values):
    width = values.shape[1]
    joined = jnp.concatenate(split(values), axis=1)
    result = dot(table, jnp.concatenate([joined, joined], axis=0))
    return result[:, :width] + result[:, width:]


def two_planes(table, values):
    high, low = split(jnp.concatenate(values, axis=1))
    return dot(table, jnp.concatenate([high, high, low], axis=0))


def first_frequencies(folded, sums, diffs, table):
    count, width = planes[0].rows, folded.shape[1] // 2
    spans = [slice(i * count, (i + 1) * count) for i in range(2)]
    even = two_planes(table[0], [folded[rows, :width] for rows in spans])
    odd = two_planes(table[1], [folded[rows, width:] for rows in spans])
    found = []
    for i, rows in enumerate(spans):
        lanes = slice(i * width, (i + 1) * width)
        found.append(multiplied(even[:, lanes], odd[:, lanes], sums[rows, :], diffs[rows, :]))
    return [jnp.concatenate(pair, axis=1) for pair in zip(*found)]


def last_frequencies(bands, folded, sums, diffs, table):
    plane = planes[2]
    rows, edge = pl.ds(plane.row, plane.rows), ceil_to(HALO_CH + 1, 16)
    both = folded[rows, :]
    width = both.shape[1] // 2
    both = jnp.concatenate([both[:edge] + dot(one_hot(edge, plane.row, bands[0]), bands[1]), both[edge:]], axis=0)
    even, odd = one_plane(table[0], both[:, :width]), one_plane(table[1], both[:, width:])
    return multiplied(even, odd, sums[rows, :], diffs[rows, :])


def put_first(result, total, gap, table):
    width, straight = result.shape[1], planes[0].count // 2
    cosine, sine = two_planes(table[0], [total]), two_planes(table[1], [gap])
    lower = cosine + sine
    high, low = split(cosine - sine)
    upper = backwards(
        straight, planes[0].half, high.shape[0],
        lambda matrix, first, stop: dot(matrix, high[first:stop]) + dot(matrix, low[first:stop]),
    )
    for i in range(2):
        lanes, start = slice(i * width, (i + 1) * width), planes[i].wire
        result[start : start + straight, :] = lower[:straight, lanes]
        result[start + straight : start + 2 * straight, :] = upper[:, lanes]


def put_last(result, total, gap, table):
    plane = planes[2]
    width, straight = result.shape[1], plane.count // 2
    cosine, sine = one_plane(table[0, plane.keep :], total), one_plane(table[1, plane.keep :], gap)
    result[:straight, :] = (cosine + sine)[:straight]
    back = jnp.concatenate(split(cosine - sine), axis=1)
    turned = backwards(
        straight, plane.half - plane.keep, back.shape[0], lambda matrix, first, stop: dot(matrix, back[first:stop])
    )
    result[straight:, :] = turned[:, :width] + turned[:, width:]


def far_part(parts, *refs):
    received, (chosen, far_signs, near, folded) = refs[:parts], refs[parts:]
    operand = fold_operand(jnp.concatenate([ref[...] for ref in received], axis=0), far_signs[...])
    folded[...] = near[...] + dot(chosen[...], operand)


def all_planes(blocks, share, neighbours, *refs):
    halo = refs[: blocks + 1]
    folded, sums, diffs, narrow, wide, own = refs[blocks + 1 : blocks + 7]
    sends, result = refs[blocks + 7 : 2 * blocks + 6], refs[2 * blocks + 6]
    last = planes[2]
    put_first(result, *first_frequencies(folded, sums, diffs, narrow), narrow)
    parts = last_frequencies(halo_operand(blocks, neighbours, halo), folded, sums, diffs, wide)
    put_last(result.at[pl.ds(last.wire, last.count)], *parts, wide)
    here = lax.axis_index("chan")
    own[...] = result[pl.ds(pl.multiple_of(here * share, share), share), :]
    for shift, out in enumerate(sends, 1):
        first = pl.multiple_of(lax.rem(here + shift, blocks) * share, share)
        out[...] = result[pl.ds(first, share), :].astype(bf16)


def leading_planes(neighbours, halo0, halo1, halo2, folded, sums, diffs, narrow, wide, send, rest, result):
    last = planes[2]
    count = send.shape[0]

    @pl.when(lax.axis_index("chan") == 0)
    def _():
        bands = halo_operand(2, neighbours, (halo0, halo1, halo2))
        put_last(result.at[: last.count], *last_frequencies(bands, folded, sums, diffs, wide), wide)
        left = last.count - count
        send[...] = result[left : last.count, :].astype(bf16)
        rest[:left, :] = result[:left, :]

    @pl.when(lax.axis_index("chan") != 0)
    def _():
        put_first(result, *first_frequencies(folded, sums, diffs, narrow), narrow)
        send[...] = result[:count, :].astype(bf16)
        rest[...] = result[count:, :]


def trailing_planes(neighbours, halo0, halo1, halo2, folded, sums, diffs, narrow, wide, rest, send, own, result):
    count, share, last = send.shape[0], own.shape[0], planes[2]

    @pl.when(lax.axis_index("chan") == 0)
    def _():
        put_first(result, *first_frequencies(folded, sums, diffs, narrow), narrow)
        own[...] = result[:share, :]
        left = result.shape[0] - share
        send[:left, :] = result[share:, :].astype(bf16)
        send[left:, :] = rest[: count - left, :].astype(bf16)

    @pl.when(lax.axis_index("chan") != 0)
    def _():
        above = share - last.count
        bands = halo_operand(2, neighbours, (halo0, halo1, halo2))
        put_last(own.at[pl.ds(above, last.count)], *last_frequencies(bands, folded, sums, diffs, wide), wide)
        own[:above, :] = rest[count:, :]
        send[...] = rest[:count, :].astype(bf16)


def spread_mask(mask, share, ticks):
    marked = jnp.where(mask == 1, 1.0, 0.0).astype(bf16)
    row = lax.broadcasted_iota(jnp.int32, (share, mask.shape[1]), 0)
    column = lax.broadcasted_iota(jnp.int32, (share, mask.shape[1]), 1)
    taken = jnp.where(row // BC == column, 1.0, 0.0).astype(bf16)
    rows = lax.dot_general(taken, marked, (((1,), (1,)), ((), ())), preferred_element_type=f32).astype(bf16)
    row = lax.broadcasted_iota(jnp.int32, (mask.shape[0], ticks), 0)
    column = lax.broadcasted_iota(jnp.int32, (mask.shape[0], ticks), 1)
    return dot(rows, jnp.where(column // BT == row, 1.0, 0.0).astype(bf16))


def chosen_signal(both, inside):
    ticks = inside.shape[1]
    return jnp.where(inside > 0.5, both[:, :ticks], both[:, ticks:])


def scaled_basis(block, blocks, basis, filters, harmonics):
    padded = basis.shape[1] // 2
    ticks = basis.shape[2]
    gains = []
    for gain in filters:
        columns = gain[...] if blocks == 1 else None
        for b in range(blocks):
            piece = gain[:, b * harmonics : (b + 1) * harmonics]
            columns = piece if columns is None else jnp.where(block == b, piece, columns)
        if padded > harmonics:
            columns = jnp.concatenate([columns, jnp.zeros((1, padded - harmonics), f32)], axis=1)
        columns = jnp.concatenate([columns, columns], axis=1)
        tall = jnp.transpose(jnp.broadcast_to(columns, (lane, 2 * padded)))
        gains.append(jnp.concatenate([tall] * (ticks // lane), axis=1))
    values = basis[block]
    return split(jnp.concatenate([values * part for part in gains], axis=1))


def own_signal(blocks, own, basis_source, wide_filter, tight_filter, mask, signal, bases, inside, basis, sem):
    basis_copy = pltpu.make_async_copy(basis_source, basis, sem)
    basis_copy.start()
    inside[...] = spread_mask(mask[...], own.shape[0], signal.shape[1])
    basis_copy.wait()
    here = lax.axis_index("chan")
    ticks = signal.shape[1]
    harmonics = wide_filter.shape[1] // blocks
    filters = (wide_filter, tight_filter)
    high, low = scaled_basis(here, blocks, basis, filters, harmonics)
    joined = jnp.concatenate(split(own[...]), axis=1)
    both = dot(joined, jnp.concatenate([high, high], axis=0))
    both += dot(joined, jnp.concatenate([low, low], axis=0))
    signal[...] = chosen_signal(both, inside[...])
    for shift in range(1, blocks):
        parts = scaled_basis(lax.rem(here + blocks - shift, blocks), blocks, basis, filters, harmonics)
        bases[shift - 1] = jnp.concatenate(parts, axis=0)


def whole_signal(blocks, signal, bases, inside, *refs):
    out = refs[-1]
    both = None
    for shift in range(1, blocks):
        values = refs[shift - 1][...]
        term = dot(jnp.concatenate([values, values], axis=1), bases[shift - 1])
        both = term if both is None else both + term
    if both is None:
        out[...] = signal[...]
    else:
        out[...] = signal[...] + chosen_signal(both, inside[...])


def part_signal(spans, signal, bases, inside, values, *refs):
    out, room, sems = refs[-3:]
    step = room.shape[0] // sems.shape[0]
    for device, (first, count) in enumerate(spans):

        @pl.when(lax.axis_index("chan") == device)
        def _(first=first, count=count):
            copies = []
            for i in range(count // step):
                some = values[i * step : (i + 1) * step, :]
                both = dot(jnp.concatenate([some, some], axis=1), bases[0])
                rows, slot = pl.ds(first + i * step, step), pl.ds(i * step, step)
                room[slot, :] = signal[rows, :] + chosen_signal(both, inside[rows, :])
                copies.append(pltpu.make_async_copy(room.at[slot], out.at[rows], sems.at[i]))
                copies[-1].start()
            for copy in copies:
                copy.wait()


costs = {
    "tick_spectra": 500, "edge_bands": 200, "near_part": 600, "factors": 575, "far_part": 300, "leading_planes": 850, "trailing_planes": 850,
    "own_signal": 500, "part_signal": 250, "all_planes": 2000,
}
costs = {name: cost * 1250000 for name, cost in costs.items()}


def call(kernel, outs, ins, name, scratch=(), final=False, aliases=None):
    kind = jax.ShapeDtypeStruct if final else pltpu.VMEM
    return pl.pallas_call(
        kernel,
        out_shape=[kind(shape, dtype) for shape, dtype in outs],
        in_specs=ins,
        out_specs=[pinned if final else whole] * len(outs),
        scratch_shapes=scratch,
        compiler_params=pltpu.CompilerParams(vmem_limit_bytes=28 * 1024 * 1024),
        cost_estimate=pl.CostEstimate(flops=costs[name], bytes_accessed=0, transcendentals=0),
        input_output_aliases=aliases or {},
        name=name,
    )


def body(frames, link_to_wire, neighbours, kernel, wide_filter, tight_filter, roi_mask):
    frames, roi_mask = frames[0], roi_mask[0]
    share, ticks = frames.shape
    blocks = lax.axis_size("chan")
    detectors = lax.axis_size("apa")
    padded = max(kernel.shape[1], lane // 2)
    width = 2 * padded
    wires = link_to_wire if share % lane == 0 else link_to_wire.reshape(blocks, share)
    table = jnp.asarray(forward_tables(ticks, blocks, padded))

    def around(parts):
        return [
            lax.ppermute(part, "chan", [(i, (i + s) % blocks) for i in range(blocks)])
            for s, part in enumerate(parts, 1)
        ]

    first = call(
        functools.partial(tick_spectra, blocks),
        [((share, width), bf16)] * (blocks - 1)
        + [((share, ticks), bf16), ((blocks, ticks, width), bf16), (wires.shape, jnp.int32), (neighbours.shape, jnp.int32)],
        [pinned] * 4, "tick_spectra", [pltpu.SemaphoreType.DMA((7,))],
    )(*map(distant, (frames, table, wires, neighbours)))
    frames, table, wires, neighbours = map(near, first[blocks - 1 :])
    received = list(map(near, around(first[: blocks - 1])))
    bands = call(
        functools.partial(edge_bands, blocks), [((blocks * HALO_CH, width), bf16)] * 2, [whole] * 4, "edge_bands",
    )(neighbours, frames, table, wires)
    narrow = jnp.asarray(channel_tables(planes[0].length, planes[0].rows, (0, 1, 0)))
    wide = jnp.asarray(channel_tables(planes[2].length, planes[2].rows, (0, 1)))
    sources = [kernel, narrow]
    folded, *ready = call(
        lambda *refs: near_part(refs[: len(sources)], *refs[len(sources) :]),
        [((all_rows, 2 * width), f32)] + [(part.shape, part.dtype) for part in sources],
        [pinned] * len(sources) + [whole] * 3, "near_part", [pltpu.SemaphoreType.DMA((len(sources),))],
    )(*map(distant, sources), wires, frames, table)
    halo = []
    for way, band in enumerate(bands):
        pairs = [(a, partners(a)[way]) for a in range(detectors) if 0 <= partners(a)[way] < detectors]
        halo.append(lax.ppermute(band, "apa", pairs))
    *halo, folded = lax.optimization_barrier((*halo, folded))
    shares = [
        jnp.concatenate([band[s * HALO_CH : (s + 1) * HALO_CH] for band in halo]) for s in range(1, blocks)
    ]
    halo = [near(band) for band in halo + around(shares)]
    kernel, narrow = map(near, ready)
    folded = near(folded)
    spare_rows = (blocks - 1) * share
    both = ((all_rows, 2 * width), f32)
    sums, diffs, chosen, far_signs, wide = map(near, call(
        functools.partial(factors, blocks, share),
        [both, both, ((all_rows, spare_rows), bf16), ((spare_rows, width), f32), (wide.shape, bf16)],
        [whole] * 2 + [pinned], "factors", [pltpu.SemaphoreType.DMA],
    )(kernel, wires, distant(wide)))
    (folded,) = call(
        functools.partial(far_part, blocks - 1), [both], [whole] * (blocks + 2), "far_part",
    )(*received, chosen, far_signs, folded)
    operands = (neighbours, *halo, near(folded), sums, diffs, narrow, wide)
    basis = jnp.asarray(inverse_tables(ticks, blocks, padded))
    filters = (wide_filter[None], tight_filter[None])
    mask = jnp.transpose(roi_mask)
    signal_shapes = [
        ((share, ticks), f32), ((max(blocks - 1, 1), 2 * width, 2 * ticks), bf16), ((share, ticks), f32)
    ]

    def own_part(own):
        return call(
            functools.partial(own_signal, blocks), signal_shapes,
            [whole, pinned] + [whole] * 3, "own_signal",
            [pltpu.VMEM(basis.shape, f32), pltpu.SemaphoreType.DMA],
        )(near(own), distant(basis), *filters, mask)

    if blocks != 2:
        own, *sends = call(
            functools.partial(all_planes, blocks, share),
            [((share, width), f32)] + [((share, width), bf16)] * (blocks - 1),
            [whole] * (blocks + 7), "all_planes",
            [pltpu.VMEM((CHANNELS, width), f32)],
        )(*operands)
        returned = map(near, around(sends))
        signal, bases, inside = own_part(own)
        out = pl.pallas_call(
            functools.partial(whole_signal, blocks),
            out_shape=jax.ShapeDtypeStruct((share, ticks), f32),
            in_specs=[whole] * (blocks + 2),
            out_specs=whole,
            name="whole_signal",
        )(*map(near, (signal, bases, inside)), *returned)
        return out[None]

    below, above = share - PU, PU + PV - share
    sent, rest = call(
        leading_planes, [((PU, width), bf16), ((PV, width), f32)],
        [whole] * 9, "leading_planes", [pltpu.VMEM((PU + PV, width), f32)],
    )(*operands)
    (early,) = map(near, around([sent]))
    sent, own = call(
        trailing_planes, [((below, width), bf16), ((share, width), f32)],
        [whole] * 10, "trailing_planes", [pltpu.VMEM((PU + PV, width), f32)],
    )(*operands, near(rest))
    signal, bases, inside = own_part(own)
    signal = near(signal)
    (late,) = map(near, around([sent]))

    def finish(values, spans, *before):
        step = math.gcd(PU, below)
        rows = max(count for _, count in spans)
        (out,) = call(
            functools.partial(part_signal, spans), [((share, ticks), f32)],
            [whole] * 4 + [pinned] * len(before), "part_signal",
            [pltpu.VMEM((rows, ticks), f32), pltpu.SemaphoreType.DMA((rows // step,))],
            final=True, aliases={4: 0} if before else None,
        )(signal, near(bases), near(inside), values, *before)
        return out

    out = finish(early, ((0, PU), (below, PU)))
    return finish(late, ((PU, below), (0, below)), out)[None]


def solution(mesh):
    placed = (
        P("apa", "chan", None),
        P("apa", None),
        P("apa", None),
        P(None, "chan", None),
        P(),
        P(),
        P("apa", "chan", None),
    )
    return jax.shard_map(
        body, mesh=mesh, in_specs=placed, out_specs=P("apa", "chan", None), check_vma=False
    )
```

```python
import functools
import math

import jax
import jax.numpy as jnp
import ml_dtypes
import numpy as np
from jax import lax
from jax.experimental import pallas as pl
from jax.experimental.pallas import tpu as pltpu
from jax.sharding import PartitionSpec as P

PU = 800
PV = 800
PW = 960
HALO_CH = 128
BC = 16
BT = 64
CHANNELS = 2560

two_pi = 2.0 * math.pi
lane = 128
f32 = jnp.float32
bf16 = jnp.bfloat16
whole = pl.BlockSpec(memory_space=pltpu.VMEM)
pinned = pl.BlockSpec(memory_space=pltpu.HBM)


def near(array):
    return pltpu.with_memory_space_constraint(array, pltpu.VMEM)


def distant(array):
    return pltpu.with_memory_space_constraint(array, pltpu.HBM)


def ceil_to(size, step):
    return -(-size // step) * step


class Plane:
    def __init__(self, length, wire, count, keep, kernel_start, row):
        self.length, self.wire, self.count, self.keep = length, wire, count, keep
        self.kernel_start, self.row = kernel_start, row
        self.half = length // 2
        self.rows = ceil_to(self.half + 1, 16)


def make_planes():
    found, row, start = [], 0, 0
    for length, wire, count, keep in (
        (PU, 0, PU, 0),
        (PV, PU, PV, 0),
        (PW + 2 * HALO_CH, PU + PV, PW, HALO_CH),
    ):
        found.append(Plane(length, wire, count, keep, start, row))
        row += found[-1].rows
        start += length
    return found


planes = make_planes()
all_rows = planes[-1].row + planes[-1].rows


def split(values):
    high = values.astype(bf16)
    return high, (values - high.astype(f32)).astype(bf16)


def channel_tables(length, rows, order):
    index = np.arange(rows)
    angles = (index[:, None] * index[None, :] % length) * (two_pi / length)
    inside = (index <= length // 2).astype(np.float64)
    mask = inside[:, None] * inside[None, :]
    found = []
    for values in (np.cos(angles) * mask, np.sin(angles) * mask):
        high = values.astype(np.float32).astype(ml_dtypes.bfloat16)
        low = (values - high.astype(np.float64)).astype(np.float32).astype(ml_dtypes.bfloat16)
        found.append(np.concatenate([(high, low)[i] for i in order], axis=1))
    return np.stack(found)


def tick_angles(ticks):
    return (np.arange(ticks)[:, None] * np.arange(ticks // 2)[None, :] % ticks) * (two_pi / ticks)


def in_blocks(values, blocks, padded):
    parts = np.stack(np.split(values, blocks, axis=-1))
    return np.pad(parts, [(0, 0)] * (parts.ndim - 1) + [(0, padded - parts.shape[-1])])


def forward_tables(ticks, blocks, padded):
    angles = tick_angles(ticks)
    halves = [in_blocks(part, blocks, padded) for part in (np.cos(angles), -np.sin(angles))]
    return np.concatenate(halves, axis=-1).astype(np.float32).astype(ml_dtypes.bfloat16)


def inverse_tables(ticks, blocks, padded):
    angles = tick_angles(ticks)
    weights = np.where(np.arange(ticks // 2) == 0, 1.0, 2.0) / ticks
    halves = [in_blocks(part * weights, blocks, padded) for part in (np.cos(angles), -np.sin(angles))]
    return np.ascontiguousarray(np.swapaxes(np.concatenate(halves, axis=-1), 1, 2)).astype(np.float32)


def dot(left, right):
    return jnp.dot(left, right, preferred_element_type=f32)


def one_hot(rows, first, targets):
    numbers = lax.broadcasted_iota(jnp.int16, (rows, targets.shape[1]), 0)
    return jnp.where(numbers == (targets - first).astype(jnp.int16), bf16(1), bf16(0))


def wires_of(wires, block, share):
    if wires.shape[0] > 1:
        return wires[pl.ds(block, 1), :]
    return wires[:, pl.ds(pl.multiple_of(block * share, lane), share)]


def tick_spectra(blocks, frames_source, table_source, wires_source, neighbours_source, *refs):
    outs, (frames, table, wires, neighbours, sems) = refs[: blocks - 1], refs[blocks - 1 :]
    parts = 1
    size = frames.shape[0] // parts
    spans = [pl.ds(i * size, size) for i in range(parts)]
    pairs = [(table_source, table)] + [(frames_source.at[span], frames.at[span]) for span in spans]
    pairs += [(wires_source, wires), (neighbours_source, neighbours)]
    copies = [pltpu.make_async_copy(source, target, sems.at[i]) for i, (source, target) in enumerate(pairs)]
    for copy in copies:
        copy.start()
    copies[0].wait()
    here = lax.axis_index("chan")
    for copy, span in zip(copies[1:], spans):
        copy.wait()
        for s, out in enumerate(outs, 1):
            out[span, :] = dot(frames[span, :], table[lax.rem(here + s, blocks)]).astype(bf16)
    for copy in copies[1 + parts :]:
        copy.wait()


def partners(detector):
    odd = detector % 2
    return detector + 1 - 2 * odd, detector - 1 + 2 * odd


def edge_bands(blocks, neighbours, frames, table, wires, *bands):
    here = lax.axis_index("chan")
    mine = wires_of(wires, here, frames.shape[0])
    for other, out in zip(partners(lax.axis_index("apa")), bands):
        first = jnp.where(neighbours[:, 1:2] == other, CHANNELS - HALO_CH, PU + PV)
        rows = dot(one_hot(HALO_CH, first, mine), frames[...]).astype(bf16)
        for s in range(blocks):
            spectra = dot(rows, table[lax.rem(here + s, blocks)])
            out[s * HALO_CH : (s + 1) * HALO_CH, :] = spectra.astype(bf16)


def lane_signs(width):
    return jnp.where(lax.broadcasted_iota(jnp.int32, (1, width), 1) < width // 2, 1.0, -1.0)


def rotated(values):
    width = values.shape[1]
    return pltpu.roll(values, width // 2, 1) * lane_signs(width)


def spread(values):
    width = values.shape[1]
    first = lax.broadcasted_iota(jnp.int32, values.shape, 1) < width // 2
    other = pltpu.roll(values, width // 2, 1)
    return jnp.concatenate([jnp.where(first, values, other), jnp.where(first, other, values)], axis=1)


def fold_of(offset, length, row):
    behind = 2 * offset > length
    return row + jnp.where(behind, length - offset, offset), jnp.where(behind, -1.0, 1.0)


def fold_of_wires(wires):
    first, second = wires < PU, wires < PU + PV
    offset = jnp.where(first, wires, jnp.where(second, wires - PU, wires - (PU + PV) + HALO_CH))
    length = jnp.where(first, PU, jnp.where(second, PV, planes[2].length))
    row = jnp.where(first, planes[0].row, jnp.where(second, planes[1].row, planes[2].row))
    return fold_of(offset, length, row)


def fold_of_halo(begin):
    offset = lax.broadcasted_iota(jnp.int32, (1, HALO_CH), 1) + begin
    return fold_of(offset, planes[2].length, planes[2].row)


def sign_columns(signs, width):
    return jnp.transpose(jnp.broadcast_to(signs, (width, signs.shape[1]))) * lane_signs(width)


def backwards(count, last, limit, product):
    parts = []
    for start in range(0, count, lane):
        size = min(lane, count - start)
        high, low = min(last - start, limit - 1), max(last - start - size + 1, 0)
        first = low // lane * lane
        stop = min(ceil_to(high + 1, lane), limit)
        row = lax.broadcasted_iota(jnp.int32, (size, stop - first), 0)
        column = lax.broadcasted_iota(jnp.int32, (size, stop - first), 1)
        matrix = jnp.where(column == last - start - first - row, 1.0, 0.0).astype(bf16)
        parts.append(product(matrix, first, stop))
    return jnp.concatenate(parts, axis=0)


def fold_operand(spectra, signs):
    width = spectra.shape[1]
    turned = pltpu.roll(spectra.astype(f32), width // 2, 1) * signs
    return jnp.concatenate([spectra, turned.astype(bf16)], axis=1)


def near_part(sources, wires, frames, table, folded, *refs):
    kept, sems = refs[:-1], refs[-1]
    copies = [pltpu.make_async_copy(source, target, sems.at[i]) for i, (source, target) in enumerate(zip(sources, kept))]
    for copy in copies:
        copy.start()
    here = lax.axis_index("chan")
    width = folded.shape[1] // 2
    targets, signs = fold_of_wires(wires_of(wires, here, frames.shape[0]))
    spectra = dot(frames[...], table[here])
    turned = pltpu.roll(spectra, width // 2, 1) * sign_columns(signs, width)
    operand = jnp.concatenate(split(spectra) + split(turned), axis=1)
    for plane in planes:
        rows = pl.ds(plane.row, plane.rows)
        both = dot(one_hot(plane.rows, plane.row, targets), operand)
        folded[rows, :width] = both[:, :width] + both[:, width : 2 * width]
        folded[rows, width:] = both[:, 2 * width : 3 * width] + both[:, 3 * width :]
    for copy in copies:
        copy.wait()


def factors(blocks, share, kernel, wires, wide_source, sums, diffs, chosen, far_signs, wide, sem):
    copy = pltpu.make_async_copy(wide_source, wide, sem)
    copy.start()
    harmonics, width = kernel.shape[1], sums.shape[1] // 2
    spare = width // 2 - harmonics
    for plane in planes:
        rows = pl.ds(plane.row, plane.rows)
        start = plane.kernel_start // lane * lane
        stop = ceil_to(plane.kernel_start + plane.length, lane)
        offset = plane.kernel_start - start
        parts = []
        for z in range(2):
            parts.append(kernel[z, :, start:stop])
            if spare:
                parts.append(jnp.zeros((spare, stop - start), f32))
        values = jnp.concatenate(parts, axis=0)
        direct = jnp.transpose(values[:, : ceil_to(offset + plane.rows, lane)])[offset : offset + plane.rows]
        pair = jnp.concatenate(split(values), axis=0)

        def product(matrix, first, stop):
            return lax.dot_general(
                matrix, pair[:, first:stop], (((1,), (1,)), ((), ())), preferred_element_type=f32
            )

        both = backwards(plane.rows, plane.length + offset, stop - start, product)
        mirror = (both[:, :width] + both[:, width:]) * (1.0 / plane.length)
        row = lax.broadcasted_iota(jnp.int32, (plane.rows, width), 0)
        direct = jnp.where(row <= plane.half, direct * (1.0 / plane.length), 0.0)
        mirror = jnp.where((row > 0) & (row < plane.half), mirror, 0.0)
        sums[rows, :] = spread(direct + mirror)
        diffs[rows, :] = spread(direct - mirror)
    here = lax.axis_index("chan")
    for s in range(1, blocks):
        targets, signs = fold_of_wires(wires_of(wires, lax.rem(here + blocks - s, blocks), share))
        span = pl.ds((s - 1) * share, share)
        chosen[:, span] = one_hot(all_rows, 0, targets)
        far_signs[span, :] = sign_columns(signs, width)
    copy.wait()


def multiplied(even, odd, plus, minus):
    width = even.shape[1]
    even_turned, odd_turned = rotated(even), rotated(odd)
    plus_re, plus_im, minus_re, minus_im = plus[:, :width], plus[:, width:], minus[:, :width], minus[:, width:]
    total = (even * plus_re + odd * minus_re) - (even_turned * plus_im + odd_turned * minus_im)
    gap = (even * minus_im + odd * plus_im) + (even_turned * minus_re + odd_turned * plus_re)
    return total, -gap


def halo_operand(blocks, neighbours, halo):
    bands, targets, signs = [], [], []
    lower, upper = neighbours[:, 0:1], neighbours[:, 1:2]
    never = -4 * planes[2].length
    for way, other in enumerate(partners(lax.axis_index("apa"))):
        total = halo[way][:HALO_CH, :].astype(f32)
        for ref in halo[2:]:
            total += ref[way * HALO_CH : (way + 1) * HALO_CH, :].astype(f32)
        bands.append(total.astype(bf16))
        begin = jnp.where(upper == other, planes[2].length - HALO_CH, never)
        begin = jnp.where(lower == other, 0, begin)
        target, sign = fold_of_halo(jnp.where(other < 0, never, begin))
        targets.append(target)
        signs.append(sign)
    signs = sign_columns(jnp.concatenate(signs, axis=1), bands[0].shape[1])
    operand = fold_operand(jnp.concatenate(bands, axis=0), signs)
    return jnp.concatenate(targets, axis=1), operand


def one_plane(table, values):
    width = values.shape[1]
    joined = jnp.concatenate(split(values), axis=1)
    result = dot(table, jnp.concatenate([joined, joined], axis=0))
    return result[:, :width] + result[:, width:]


def two_planes(table, values):
    high, low = split(jnp.concatenate(values, axis=1))
    return dot(table, jnp.concatenate([high, high, low], axis=0))


def first_frequencies(folded, sums, diffs, table):
    count, width = planes[0].rows, folded.shape[1] // 2
    spans = [slice(i * count, (i + 1) * count) for i in range(2)]
    even = two_planes(table[0], [folded[rows, :width] for rows in spans])
    odd = two_planes(table[1], [folded[rows, width:] for rows in spans])
    found = []
    for i, rows in enumerate(spans):
        lanes = slice(i * width, (i + 1) * width)
        found.append(multiplied(even[:, lanes], odd[:, lanes], sums[rows, :], diffs[rows, :]))
    return [jnp.concatenate(pair, axis=1) for pair in zip(*found)]


def last_frequencies(bands, folded, sums, diffs, table):
    plane = planes[2]
    rows, edge = pl.ds(plane.row, plane.rows), ceil_to(HALO_CH + 1, 16)
    both = folded[rows, :]
    width = both.shape[1] // 2
    both = jnp.concatenate([both[:edge] + dot(one_hot(edge, plane.row, bands[0]), bands[1]), both[edge:]], axis=0)
    even, odd = one_plane(table[0], both[:, :width]), one_plane(table[1], both[:, width:])
    return multiplied(even, odd, sums[rows, :], diffs[rows, :])


def put_first(result, total, gap, table):
    width, straight = result.shape[1], planes[0].count // 2
    cosine, sine = two_planes(table[0], [total]), two_planes(table[1], [gap])
    lower = cosine + sine
    high, low = split(cosine - sine)
    upper = backwards(
        straight, planes[0].half, high.shape[0],
        lambda matrix, first, stop: dot(matrix, high[first:stop]) + dot(matrix, low[first:stop]),
    )
    for i in range(2):
        lanes, start = slice(i * width, (i + 1) * width), planes[i].wire
        result[start : start + straight, :] = lower[:straight, lanes]
        result[start + straight : start + 2 * straight, :] = upper[:, lanes]


def put_last(result, total, gap, table):
    plane = planes[2]
    width, straight = result.shape[1], plane.count // 2
    cosine, sine = one_plane(table[0, plane.keep :], total), one_plane(table[1, plane.keep :], gap)
    result[:straight, :] = (cosine + sine)[:straight]
    back = jnp.concatenate(split(cosine - sine), axis=1)
    turned = backwards(
        straight, plane.half - plane.keep, back.shape[0], lambda matrix, first, stop: dot(matrix, back[first:stop])
    )
    result[straight:, :] = turned[:, :width] + turned[:, width:]


def far_part(parts, *refs):
    received, (chosen, far_signs, near, folded) = refs[:parts], refs[parts:]
    operand = fold_operand(jnp.concatenate([ref[...] for ref in received], axis=0), far_signs[...])
    folded[...] = near[...] + dot(chosen[...], operand)


def all_planes(blocks, share, neighbours, *refs):
    halo = refs[: blocks + 1]
    folded, sums, diffs, narrow, wide, own = refs[blocks + 1 : blocks + 7]
    sends, result = refs[blocks + 7 : 2 * blocks + 6], refs[2 * blocks + 6]
    last = planes[2]
    put_first(result, *first_frequencies(folded, sums, diffs, narrow), narrow)
    parts = last_frequencies(halo_operand(blocks, neighbours, halo), folded, sums, diffs, wide)
    put_last(result.at[pl.ds(last.wire, last.count)], *parts, wide)
    here = lax.axis_index("chan")
    own[...] = result[pl.ds(pl.multiple_of(here * share, share), share), :]
    for shift, out in enumerate(sends, 1):
        first = pl.multiple_of(lax.rem(here + shift, blocks) * share, share)
        out[...] = result[pl.ds(first, share), :].astype(bf16)


def leading_planes(neighbours, halo0, halo1, halo2, folded, sums, diffs, narrow, wide, send, rest, result):
    last = planes[2]
    count = send.shape[0]

    @pl.when(lax.axis_index("chan") == 0)
    def _():
        bands = halo_operand(2, neighbours, (halo0, halo1, halo2))
        put_last(result.at[: last.count], *last_frequencies(bands, folded, sums, diffs, wide), wide)
        left = last.count - count
        send[...] = result[left : last.count, :].astype(bf16)
        rest[:left, :] = result[:left, :]

    @pl.when(lax.axis_index("chan") != 0)
    def _():
        put_first(result, *first_frequencies(folded, sums, diffs, narrow), narrow)
        send[...] = result[:count, :].astype(bf16)
        rest[...] = result[count:, :]


def trailing_planes(neighbours, halo0, halo1, halo2, folded, sums, diffs, narrow, wide, rest, send, own, result):
    count, share, last = send.shape[0], own.shape[0], planes[2]

    @pl.when(lax.axis_index("chan") == 0)
    def _():
        put_first(result, *first_frequencies(folded, sums, diffs, narrow), narrow)
        own[...] = result[:share, :]
        left = result.shape[0] - share
        send[:left, :] = result[share:, :].astype(bf16)
        send[left:, :] = rest[: count - left, :].astype(bf16)

    @pl.when(lax.axis_index("chan") != 0)
    def _():
        above = share - last.count
        bands = halo_operand(2, neighbours, (halo0, halo1, halo2))
        put_last(own.at[pl.ds(above, last.count)], *last_frequencies(bands, folded, sums, diffs, wide), wide)
        own[:above, :] = rest[count:, :]
        send[...] = rest[:count, :].astype(bf16)


def spread_mask(mask, share, ticks):
    marked = jnp.where(mask == 1, 1.0, 0.0).astype(bf16)
    row = lax.broadcasted_iota(jnp.int32, (share, mask.shape[1]), 0)
    column = lax.broadcasted_iota(jnp.int32, (share, mask.shape[1]), 1)
    taken = jnp.where(row // BC == column, 1.0, 0.0).astype(bf16)
    rows = lax.dot_general(taken, marked, (((1,), (1,)), ((), ())), preferred_element_type=f32).astype(bf16)
    row = lax.broadcasted_iota(jnp.int32, (mask.shape[0], ticks), 0)
    column = lax.broadcasted_iota(jnp.int32, (mask.shape[0], ticks), 1)
    return dot(rows, jnp.where(column // BT == row, 1.0, 0.0).astype(bf16))


def chosen_signal(both, inside):
    ticks = inside.shape[1]
    return jnp.where(inside > 0.5, both[:, :ticks], both[:, ticks:])


def scaled_basis(block, blocks, basis, filters, harmonics):
    padded = basis.shape[1] // 2
    ticks = basis.shape[2]
    gains = []
    for gain in filters:
        columns = gain[...] if blocks == 1 else None
        for b in range(blocks):
            piece = gain[:, b * harmonics : (b + 1) * harmonics]
            columns = piece if columns is None else jnp.where(block == b, piece, columns)
        if padded > harmonics:
            columns = jnp.concatenate([columns, jnp.zeros((1, padded - harmonics), f32)], axis=1)
        columns = jnp.concatenate([columns, columns], axis=1)
        tall = jnp.transpose(jnp.broadcast_to(columns, (lane, 2 * padded)))
        gains.append(jnp.concatenate([tall] * (ticks // lane), axis=1))
    values = basis[block]
    return split(jnp.concatenate([values * part for part in gains], axis=1))


def own_signal(blocks, own, basis_source, wide_filter, tight_filter, mask, signal, bases, inside, basis, sem):
    basis_copy = pltpu.make_async_copy(basis_source, basis, sem)
    basis_copy.start()
    inside[...] = spread_mask(mask[...], own.shape[0], signal.shape[1])
    basis_copy.wait()
    here = lax.axis_index("chan")
    ticks = signal.shape[1]
    harmonics = wide_filter.shape[1] // blocks
    filters = (wide_filter, tight_filter)
    high, low = scaled_basis(here, blocks, basis, filters, harmonics)
    joined = jnp.concatenate(split(own[...]), axis=1)
    both = dot(joined, jnp.concatenate([high, high], axis=0))
    both += dot(joined, jnp.concatenate([low, low], axis=0))
    signal[...] = chosen_signal(both, inside[...])
    for shift in range(1, blocks):
        parts = scaled_basis(lax.rem(here + blocks - shift, blocks), blocks, basis, filters, harmonics)
        bases[shift - 1] = jnp.concatenate(parts, axis=0)


def whole_signal(blocks, signal, bases, inside, *refs):
    out = refs[-1]
    both = None
    for shift in range(1, blocks):
        values = refs[shift - 1][...]
        term = dot(jnp.concatenate([values, values], axis=1), bases[shift - 1])
        both = term if both is None else both + term
    if both is None:
        out[...] = signal[...]
    else:
        out[...] = signal[...] + chosen_signal(both, inside[...])


def part_signal(spans, signal, bases, inside, values, *refs):
    out, room, sems = refs[-3:]
    step = room.shape[0] // sems.shape[0]
    for device, (first, count) in enumerate(spans):

        @pl.when(lax.axis_index("chan") == device)
        def _(first=first, count=count):
            copies = []
            for i in range(count // step):
                some = values[i * step : (i + 1) * step, :]
                both = dot(jnp.concatenate([some, some], axis=1), bases[0])
                rows, slot = pl.ds(first + i * step, step), pl.ds(i * step, step)
                room[slot, :] = signal[rows, :] + chosen_signal(both, inside[rows, :])
                copies.append(pltpu.make_async_copy(room.at[slot], out.at[rows], sems.at[i]))
                copies[-1].start()
            for copy in copies:
                copy.wait()


costs = {
    "tick_spectra": 500, "edge_bands": 200, "near_part": 600, "factors": 575, "far_part": 300, "leading_planes": 850, "trailing_planes": 850,
    "own_signal": 500, "part_signal": 250, "all_planes": 2000,
}
costs = {name: cost * 1250000 for name, cost in costs.items()}


def call(kernel, outs, ins, name, scratch=(), final=False, aliases=None):
    kind = jax.ShapeDtypeStruct if final else pltpu.VMEM
    return pl.pallas_call(
        kernel,
        out_shape=[kind(shape, dtype) for shape, dtype in outs],
        in_specs=ins,
        out_specs=[pinned if final else whole] * len(outs),
        scratch_shapes=scratch,
        compiler_params=pltpu.CompilerParams(vmem_limit_bytes=28 * 1024 * 1024),
        cost_estimate=pl.CostEstimate(flops=costs[name], bytes_accessed=0, transcendentals=0),
        input_output_aliases=aliases or {},
        name=name,
    )


def body(frames, link_to_wire, neighbours, kernel, wide_filter, tight_filter, roi_mask):
    frames, roi_mask = frames[0], roi_mask[0]
    share, ticks = frames.shape
    blocks = lax.axis_size("chan")
    detectors = lax.axis_size("apa")
    padded = max(kernel.shape[1], lane // 2)
    width = 2 * padded
    wires = link_to_wire if share % lane == 0 else link_to_wire.reshape(blocks, share)
    table = jnp.asarray(forward_tables(ticks, blocks, padded))

    def around(parts):
        return [
            lax.ppermute(part, "chan", [(i, (i + s) % blocks) for i in range(blocks)])
            for s, part in enumerate(parts, 1)
        ]

    first = call(
        functools.partial(tick_spectra, blocks),
        [((share, width), bf16)] * (blocks - 1)
        + [((share, ticks), bf16), ((blocks, ticks, width), bf16), (wires.shape, jnp.int32), (neighbours.shape, jnp.int32)],
        [pinned] * 4, "tick_spectra", [pltpu.SemaphoreType.DMA((7,))],
    )(*map(distant, (frames, table, wires, neighbours)))
    frames, table, wires, neighbours = map(near, first[blocks - 1 :])
    received = list(map(near, around(first[: blocks - 1])))
    bands = call(
        functools.partial(edge_bands, blocks), [((blocks * HALO_CH, width), bf16)] * 2, [whole] * 4, "edge_bands",
    )(neighbours, frames, table, wires)
    narrow = jnp.asarray(channel_tables(planes[0].length, planes[0].rows, (0, 1, 0)))
    wide = jnp.asarray(channel_tables(planes[2].length, planes[2].rows, (0, 1)))
    sources = [kernel, narrow]
    folded, *ready = call(
        lambda *refs: near_part(refs[: len(sources)], *refs[len(sources) :]),
        [((all_rows, 2 * width), f32)] + [(part.shape, part.dtype) for part in sources],
        [pinned] * len(sources) + [whole] * 3, "near_part", [pltpu.SemaphoreType.DMA((len(sources),))],
    )(*map(distant, sources), wires, frames, table)
    halo = []
    for way, band in enumerate(bands):
        pairs = [(a, partners(a)[way]) for a in range(detectors) if 0 <= partners(a)[way] < detectors]
        halo.append(lax.ppermute(band, "apa", pairs))
    *halo, folded = lax.optimization_barrier((*halo, folded))
    shares = [
        jnp.concatenate([band[s * HALO_CH : (s + 1) * HALO_CH] for band in halo]) for s in range(1, blocks)
    ]
    halo = [near(band) for band in halo + around(shares)]
    kernel, narrow = map(near, ready)
    folded = near(folded)
    spare_rows = (blocks - 1) * share
    both = ((all_rows, 2 * width), f32)
    sums, diffs, chosen, far_signs, wide = map(near, call(
        functools.partial(factors, blocks, share),
        [both, both, ((all_rows, spare_rows), bf16), ((spare_rows, width), f32), (wide.shape, bf16)],
        [whole] * 2 + [pinned], "factors", [pltpu.SemaphoreType.DMA],
    )(kernel, wires, distant(wide)))
    (folded,) = call(
        functools.partial(far_part, blocks - 1), [both], [whole] * (blocks + 2), "far_part",
    )(*received, chosen, far_signs, folded)
    operands = (neighbours, *halo, near(folded), sums, diffs, narrow, wide)
    basis = jnp.asarray(inverse_tables(ticks, blocks, padded))
    filters = (wide_filter[None], tight_filter[None])
    mask = jnp.transpose(roi_mask)
    signal_shapes = [
        ((share, ticks), f32), ((max(blocks - 1, 1), 2 * width, 2 * ticks), bf16), ((share, ticks), f32)
    ]

    def own_part(own):
        return call(
            functools.partial(own_signal, blocks), signal_shapes,
            [whole, pinned] + [whole] * 3, "own_signal",
            [pltpu.VMEM(basis.shape, f32), pltpu.SemaphoreType.DMA],
        )(near(own), distant(basis), *filters, mask)

    if blocks != 2:
        own, *sends = call(
            functools.partial(all_planes, blocks, share),
            [((share, width), f32)] + [((share, width), bf16)] * (blocks - 1),
            [whole] * (blocks + 7), "all_planes",
            [pltpu.VMEM((CHANNELS, width), f32)],
        )(*operands)
        returned = map(near, around(sends))
        signal, bases, inside = own_part(own)
        out = pl.pallas_call(
            functools.partial(whole_signal, blocks),
            out_shape=jax.ShapeDtypeStruct((share, ticks), f32),
            in_specs=[whole] * (blocks + 2),
            out_specs=whole,
            name="whole_signal",
        )(*map(near, (signal, bases, inside)), *returned)
        return out[None]

    below, above = share - PU, PU + PV - share
    sent, rest = call(
        leading_planes, [((PU, width), bf16), ((PV, width), f32)],
        [whole] * 9, "leading_planes", [pltpu.VMEM((PU + PV, width), f32)],
    )(*operands)
    (early,) = map(near, around([sent]))
    sent, own = call(
        trailing_planes, [((below, width), bf16), ((share, width), f32)],
        [whole] * 10, "trailing_planes", [pltpu.VMEM((PU + PV, width), f32)],
    )(*operands, near(rest))
    signal, bases, inside = own_part(own)
    signal = near(signal)
    (late,) = map(near, around([sent]))

    def finish(values, spans, *before):
        step = values.shape[0] // 2
        rows = max(count for _, count in spans)
        (out,) = call(
            functools.partial(part_signal, spans), [((share, ticks), f32)],
            [whole] * 4 + [pinned] * len(before), "part_signal",
            [pltpu.VMEM((rows, ticks), f32), pltpu.SemaphoreType.DMA((rows // step,))],
            final=True, aliases={4: 0} if before else None,
        )(signal, near(bases), near(inside), values, *before)
        return out

    out = finish(early, ((0, PU), (below, PU)))
    return finish(late, ((PU, below), (0, below)), out)[None]


def solution(mesh):
    placed = (
        P("apa", "chan", None),
        P("apa", None),
        P("apa", None),
        P(None, "chan", None),
        P(),
        P(),
        P("apa", "chan", None),
    )
    return jax.shard_map(
        body, mesh=mesh, in_specs=placed, out_specs=P("apa", "chan", None), check_vma=False
    )
```

```python
import functools
import math

import jax
import jax.numpy as jnp
import ml_dtypes
import numpy as np
from jax import lax
from jax.experimental import pallas as pl
from jax.experimental.pallas import tpu as pltpu
from jax.sharding import PartitionSpec as P

PU = 800
PV = 800
PW = 960
HALO_CH = 128
BC = 16
BT = 64
CHANNELS = 2560

two_pi = 2.0 * math.pi
lane = 128
f32 = jnp.float32
bf16 = jnp.bfloat16
whole = pl.BlockSpec(memory_space=pltpu.VMEM)
pinned = pl.BlockSpec(memory_space=pltpu.HBM)


def near(array):
    return pltpu.with_memory_space_constraint(array, pltpu.VMEM)


def distant(array):
    return pltpu.with_memory_space_constraint(array, pltpu.HBM)


def ceil_to(size, step):
    return -(-size // step) * step


class Plane:
    def __init__(self, length, wire, count, keep, kernel_start, row):
        self.length, self.wire, self.count, self.keep = length, wire, count, keep
        self.kernel_start, self.row = kernel_start, row
        self.half = length // 2
        self.rows = ceil_to(self.half + 1, 16)


def make_planes():
    found, row, start = [], 0, 0
    for length, wire, count, keep in (
        (PU, 0, PU, 0),
        (PV, PU, PV, 0),
        (PW + 2 * HALO_CH, PU + PV, PW, HALO_CH),
    ):
        found.append(Plane(length, wire, count, keep, start, row))
        row += found[-1].rows
        start += length
    return found


planes = make_planes()
edge = slice(0, ceil_to(HALO_CH + 1, 16) + 32)
inner = slice(edge.stop, planes[2].rows)
all_rows = planes[-1].row + planes[-1].rows


def split(values):
    high = values.astype(bf16)
    return high, (values - high.astype(f32)).astype(bf16)


def channel_tables(length, rows, order):
    index = np.arange(rows)
    angles = (index[:, None] * index[None, :] % length) * (two_pi / length)
    inside = (index <= length // 2).astype(np.float64)
    mask = inside[:, None] * inside[None, :]
    found = []
    for values in (np.cos(angles) * mask, np.sin(angles) * mask):
        high = values.astype(np.float32).astype(ml_dtypes.bfloat16)
        low = (values - high.astype(np.float64)).astype(np.float32).astype(ml_dtypes.bfloat16)
        found.append(np.concatenate([(high, low)[i][:, columns] for i, columns in order], axis=1))
    return np.stack(found)


def tick_angles(ticks):
    return (np.arange(ticks)[:, None] * np.arange(ticks // 2)[None, :] % ticks) * (two_pi / ticks)


def in_blocks(values, blocks, padded):
    parts = np.stack(np.split(values, blocks, axis=-1))
    return np.pad(parts, [(0, 0)] * (parts.ndim - 1) + [(0, padded - parts.shape[-1])])


def forward_tables(ticks, blocks, padded):
    angles = tick_angles(ticks)
    halves = [in_blocks(part, blocks, padded) for part in (np.cos(angles), -np.sin(angles))]
    return np.concatenate(halves, axis=-1).astype(np.float32).astype(ml_dtypes.bfloat16)


def inverse_tables(ticks, blocks, padded):
    angles = tick_angles(ticks)
    weights = np.where(np.arange(ticks // 2) == 0, 1.0, 2.0) / ticks
    halves = [in_blocks(part * weights, blocks, padded) for part in (np.cos(angles), -np.sin(angles))]
    return np.ascontiguousarray(np.swapaxes(np.concatenate(halves, axis=-1), 1, 2)).astype(np.float32)


def dot(left, right):
    return jnp.dot(left, right, preferred_element_type=f32)


def one_hot(rows, first, targets):
    numbers = lax.broadcasted_iota(jnp.int16, (rows, targets.shape[1]), 0)
    return jnp.where(numbers == (targets - first).astype(jnp.int16), bf16(1), bf16(0))


def wires_of(wires, block, share):
    if wires.shape[0] > 1:
        return wires[pl.ds(block, 1), :]
    return wires[:, pl.ds(pl.multiple_of(block * share, lane), share)]


def tick_spectra(blocks, frames_source, table_source, wires_source, neighbours_source, *refs):
    outs, (frames, table, wires, neighbours, sems) = refs[: blocks - 1], refs[blocks - 1 :]
    parts = 1
    size = frames.shape[0] // parts
    spans = [pl.ds(i * size, size) for i in range(parts)]
    pairs = [(table_source, table)] + [(frames_source.at[span], frames.at[span]) for span in spans]
    pairs += [(wires_source, wires), (neighbours_source, neighbours)]
    copies = [pltpu.make_async_copy(source, target, sems.at[i]) for i, (source, target) in enumerate(pairs)]
    for copy in copies:
        copy.start()
    copies[0].wait()
    here = lax.axis_index("chan")
    for copy, span in zip(copies[1:], spans):
        copy.wait()
        for s, out in enumerate(outs, 1):
            out[span, :] = dot(frames[span, :], table[lax.rem(here + s, blocks)]).astype(bf16)
    for copy in copies[1 + parts :]:
        copy.wait()


def partners(detector):
    odd = detector % 2
    return detector + 1 - 2 * odd, detector - 1 + 2 * odd


def edge_bands(blocks, neighbours, frames, table, wires, *bands):
    here = lax.axis_index("chan")
    mine = wires_of(wires, here, frames.shape[0])
    for other, out in zip(partners(lax.axis_index("apa")), bands):
        first = jnp.where(neighbours[:, 1:2] == other, CHANNELS - HALO_CH, PU + PV)
        rows = dot(one_hot(HALO_CH, first, mine), frames[...]).astype(bf16)
        for s in range(blocks):
            spectra = dot(rows, table[lax.rem(here + s, blocks)])
            out[s * HALO_CH : (s + 1) * HALO_CH, :] = spectra.astype(bf16)


def lane_signs(width):
    return jnp.where(lax.broadcasted_iota(jnp.int32, (1, width), 1) < width // 2, 1.0, -1.0)


def rotated(values):
    width = values.shape[1]
    return pltpu.roll(values, width // 2, 1) * lane_signs(width)


def spread(values):
    width = values.shape[1]
    first = lax.broadcasted_iota(jnp.int32, values.shape, 1) < width // 2
    other = pltpu.roll(values, width // 2, 1)
    return jnp.concatenate([jnp.where(first, values, other), jnp.where(first, other, values)], axis=1)


def fold_of(offset, length, row):
    behind = 2 * offset > length
    return row + jnp.where(behind, length - offset, offset), jnp.where(behind, -1.0, 1.0)


def fold_of_wires(wires):
    first, second = wires < PU, wires < PU + PV
    offset = jnp.where(first, wires, jnp.where(second, wires - PU, wires - (PU + PV) + HALO_CH))
    length = jnp.where(first, PU, jnp.where(second, PV, planes[2].length))
    row = jnp.where(first, planes[0].row, jnp.where(second, planes[1].row, planes[2].row))
    return fold_of(offset, length, row)


def fold_of_halo(begin):
    offset = lax.broadcasted_iota(jnp.int32, (1, HALO_CH), 1) + begin
    return fold_of(offset, planes[2].length, planes[2].row)


def sign_columns(signs, width):
    return jnp.transpose(jnp.broadcast_to(signs, (width, signs.shape[1]))) * lane_signs(width)


def backwards(count, last, limit, product):
    parts = []
    for start in range(0, count, lane):
        size = min(lane, count - start)
        high, low = min(last - start, limit - 1), max(last - start - size + 1, 0)
        first = low // lane * lane
        stop = min(ceil_to(high + 1, lane), limit)
        row = lax.broadcasted_iota(jnp.int32, (size, stop - first), 0)
        column = lax.broadcasted_iota(jnp.int32, (size, stop - first), 1)
        matrix = jnp.where(column == last - start - first - row, 1.0, 0.0).astype(bf16)
        parts.append(product(matrix, first, stop))
    return jnp.concatenate(parts, axis=0)


def fold_operand(spectra, signs):
    width = spectra.shape[1]
    turned = pltpu.roll(spectra.astype(f32), width // 2, 1) * signs
    return jnp.concatenate([spectra, turned.astype(bf16)], axis=1)


def near_part(sources, wires, frames, table, folded, *refs):
    kept, sems = refs[:-1], refs[-1]
    copies = [pltpu.make_async_copy(source, target, sems.at[i]) for i, (source, target) in enumerate(zip(sources, kept))]
    for copy in copies:
        copy.start()
    here = lax.axis_index("chan")
    width = folded.shape[1] // 2
    targets, signs = fold_of_wires(wires_of(wires, here, frames.shape[0]))
    spectra = dot(frames[...], table[here])
    turned = pltpu.roll(spectra, width // 2, 1) * sign_columns(signs, width)
    operand = jnp.concatenate(split(spectra) + split(turned), axis=1)
    for plane in planes:
        rows = pl.ds(plane.row, plane.rows)
        both = dot(one_hot(plane.rows, plane.row, targets), operand)
        folded[rows, :width] = both[:, :width] + both[:, width : 2 * width]
        folded[rows, width:] = both[:, 2 * width : 3 * width] + both[:, 3 * width :]
    for copy in copies:
        copy.wait()


def factors(blocks, share, kernel, wires, table_source, sums, diffs, chosen, far_signs, table, sem):
    copy = pltpu.make_async_copy(table_source, table, sem)
    copy.start()
    harmonics, width = kernel.shape[1], sums.shape[1] // 2
    spare = width // 2 - harmonics
    for plane in planes:
        rows = pl.ds(plane.row, plane.rows)
        start = plane.kernel_start // lane * lane
        stop = ceil_to(plane.kernel_start + plane.length, lane)
        offset = plane.kernel_start - start
        parts = []
        for z in range(2):
            parts.append(kernel[z, :, start:stop])
            if spare:
                parts.append(jnp.zeros((spare, stop - start), f32))
        values = jnp.concatenate(parts, axis=0)
        direct = jnp.transpose(values[:, : ceil_to(offset + plane.rows, lane)])[offset : offset + plane.rows]
        pair = jnp.concatenate(split(values), axis=0)

        def product(matrix, first, stop):
            return lax.dot_general(
                matrix, pair[:, first:stop], (((1,), (1,)), ((), ())), preferred_element_type=f32
            )

        both = backwards(plane.rows, plane.length + offset, stop - start, product)
        mirror = (both[:, :width] + both[:, width:]) * (1.0 / plane.length)
        row = lax.broadcasted_iota(jnp.int32, (plane.rows, width), 0)
        direct = jnp.where(row <= plane.half, direct * (1.0 / plane.length), 0.0)
        mirror = jnp.where((row > 0) & (row < plane.half), mirror, 0.0)
        sums[rows, :] = spread(direct + mirror)
        diffs[rows, :] = spread(direct - mirror)
    here = lax.axis_index("chan")
    for s in range(1, blocks):
        targets, signs = fold_of_wires(wires_of(wires, lax.rem(here + blocks - s, blocks), share))
        span = pl.ds((s - 1) * share, share)
        chosen[:, span] = one_hot(all_rows, 0, targets)
        far_signs[span, :] = sign_columns(signs, width)
    copy.wait()


def multiplied(even, odd, plus, minus):
    width = even.shape[1]
    even_turned, odd_turned = rotated(even), rotated(odd)
    plus_re, plus_im, minus_re, minus_im = plus[:, :width], plus[:, width:], minus[:, :width], minus[:, width:]
    total = (even * plus_re + odd * minus_re) - (even_turned * plus_im + odd_turned * minus_im)
    gap = (even * minus_im + odd * plus_im) + (even_turned * minus_re + odd_turned * plus_re)
    return total, -gap


def halo_operand(blocks, neighbours, halo):
    bands, targets, signs = [], [], []
    lower, upper = neighbours[:, 0:1], neighbours[:, 1:2]
    never = -4 * planes[2].length
    for way, other in enumerate(partners(lax.axis_index("apa"))):
        total = halo[way][:HALO_CH, :].astype(f32)
        for ref in halo[2:]:
            total += ref[way * HALO_CH : (way + 1) * HALO_CH, :].astype(f32)
        bands.append(total.astype(bf16))
        begin = jnp.where(upper == other, planes[2].length - HALO_CH, never)
        begin = jnp.where(lower == other, 0, begin)
        target, sign = fold_of_halo(jnp.where(other < 0, never, begin))
        targets.append(target)
        signs.append(sign)
    signs = sign_columns(jnp.concatenate(signs, axis=1), bands[0].shape[1])
    operand = fold_operand(jnp.concatenate(bands, axis=0), signs)
    return jnp.concatenate(targets, axis=1), operand


def paired(values):
    joined = jnp.concatenate(split(values), axis=1)
    return jnp.concatenate([joined, joined], axis=0)


def added(both):
    width = both.shape[1] // 2
    return both[:, :width] + both[:, width:]


def one_plane(table, values):
    return added(dot(table, jnp.concatenate([paired(values[part]) for part in (inner, edge)], axis=0)))


def inner_sums(folded, table):
    plane, width = planes[2], folded.shape[1] // 2
    both = folded[pl.ds(plane.row + inner.start, inner.stop - inner.start), :]
    stop = 2 * (inner.stop - inner.start)
    return [added(dot(table[i, :, :stop], paired(both[:, i * width : (i + 1) * width]))) for i in range(2)]


def two_planes(table, values):
    high, low = split(jnp.concatenate(values, axis=1))
    return dot(table, jnp.concatenate([high, high, low], axis=0))


def first_frequencies(folded, sums, diffs, table):
    count, width = planes[0].rows, folded.shape[1] // 2
    spans = [slice(i * count, (i + 1) * count) for i in range(2)]
    even = two_planes(table[0], [folded[rows, :width] for rows in spans])
    odd = two_planes(table[1], [folded[rows, width:] for rows in spans])
    found = []
    for i, rows in enumerate(spans):
        lanes = slice(i * width, (i + 1) * width)
        found.append(multiplied(even[:, lanes], odd[:, lanes], sums[rows, :], diffs[rows, :]))
    return [jnp.concatenate(pair, axis=1) for pair in zip(*found)]


def last_frequencies(bands, folded, sums, diffs, table, sums_of_inner=None):
    plane, width = planes[2], folded.shape[1] // 2
    rows, start = pl.ds(plane.row, plane.rows), 2 * (inner.stop - inner.start)
    both = folded[pl.ds(plane.row, edge.stop), :] + dot(one_hot(edge.stop, plane.row, bands[0]), bands[1])
    found = []
    for i, base in enumerate(sums_of_inner or inner_sums(folded, table)):
        found.append(base + added(dot(table[i, :, start:], paired(both[:, i * width : (i + 1) * width]))))
    return multiplied(*found, sums[rows, :], diffs[rows, :])


def put_first(result, total, gap, table):
    width, straight = result.shape[1], planes[0].count // 2
    cosine, sine = two_planes(table[0], [total]), two_planes(table[1], [gap])
    lower = cosine + sine
    high, low = split(cosine - sine)
    upper = backwards(
        straight, planes[0].half, high.shape[0],
        lambda matrix, first, stop: dot(matrix, high[first:stop]) + dot(matrix, low[first:stop]),
    )
    for i in range(2):
        lanes, start = slice(i * width, (i + 1) * width), planes[i].wire
        result[start : start + straight, :] = lower[:straight, lanes]
        result[start + straight : start + 2 * straight, :] = upper[:, lanes]


def put_last(result, total, gap, table):
    plane = planes[2]
    width, straight = result.shape[1], plane.count // 2
    cosine, sine = one_plane(table[0, plane.keep :], total), one_plane(table[1, plane.keep :], gap)
    result[:straight, :] = (cosine + sine)[:straight]
    back = jnp.concatenate(split(cosine - sine), axis=1)
    turned = backwards(
        straight, plane.half - plane.keep, back.shape[0], lambda matrix, first, stop: dot(matrix, back[first:stop])
    )
    result[straight:, :] = turned[:, :width] + turned[:, width:]


def far_part(parts, *refs):
    received, (chosen, far_signs, near, wide, folded, even, odd) = refs[:parts], refs[parts:]
    operand = fold_operand(jnp.concatenate([ref[...] for ref in received], axis=0), far_signs[...])
    folded[...] = near[...] + dot(chosen[...], operand)

    @pl.when((parts == 1) & (lax.axis_index("chan") == 0))
    def _():
        even[...], odd[...] = inner_sums(folded, wide)


def all_planes(blocks, share, neighbours, *refs):
    halo = refs[: blocks + 1]
    folded, sums, diffs, narrow, wide, own = refs[blocks + 1 : blocks + 7]
    sends, result = refs[blocks + 7 : 2 * blocks + 6], refs[2 * blocks + 6]
    last = planes[2]
    put_first(result, *first_frequencies(folded, sums, diffs, narrow), narrow)
    parts = last_frequencies(halo_operand(blocks, neighbours, halo), folded, sums, diffs, wide)
    put_last(result.at[pl.ds(last.wire, last.count)], *parts, wide)
    here = lax.axis_index("chan")
    own[...] = result[pl.ds(pl.multiple_of(here * share, share), share), :]
    for shift, out in enumerate(sends, 1):
        first = pl.multiple_of(lax.rem(here + shift, blocks) * share, share)
        out[...] = result[pl.ds(first, share), :].astype(bf16)


def leading_planes(neighbours, halo0, halo1, halo2, folded, sums, diffs, narrow, wide, even, odd, send, rest, result):
    last = planes[2]
    count = send.shape[0]

    @pl.when(lax.axis_index("chan") == 0)
    def _():
        bands = halo_operand(2, neighbours, (halo0, halo1, halo2))
        parts = last_frequencies(bands, folded, sums, diffs, wide, [even[...], odd[...]])
        put_last(result.at[: last.count], *parts, wide)
        left = last.count - count
        send[...] = result[left : last.count, :].astype(bf16)
        rest[:left, :] = result[:left, :]

    @pl.when(lax.axis_index("chan") != 0)
    def _():
        put_first(result, *first_frequencies(folded, sums, diffs, narrow), narrow)
        send[...] = result[:count, :].astype(bf16)
        rest[...] = result[count:, :]


def trailing_planes(neighbours, halo0, halo1, halo2, folded, sums, diffs, narrow, wide, rest, send, own, result):
    count, share, last = send.shape[0], own.shape[0], planes[2]

    @pl.when(lax.axis_index("chan") == 0)
    def _():
        put_first(result, *first_frequencies(folded, sums, diffs, narrow), narrow)
        own[...] = result[:share, :]
        left = result.shape[0] - share
        send[:left, :] = result[share:, :].astype(bf16)
        send[left:, :] = rest[: count - left, :].astype(bf16)

    @pl.when(lax.axis_index("chan") != 0)
    def _():
        above = share - last.count
        bands = halo_operand(2, neighbours, (halo0, halo1, halo2))
        put_last(own.at[pl.ds(above, last.count)], *last_frequencies(bands, folded, sums, diffs, wide), wide)
        own[:above, :] = rest[count:, :]
        send[...] = rest[:count, :].astype(bf16)


def spread_mask(mask, share, ticks):
    marked = jnp.where(mask == 1, 1.0, 0.0).astype(bf16)
    row = lax.broadcasted_iota(jnp.int32, (share, mask.shape[1]), 0)
    column = lax.broadcasted_iota(jnp.int32, (share, mask.shape[1]), 1)
    taken = jnp.where(row // BC == column, 1.0, 0.0).astype(bf16)
    rows = lax.dot_general(taken, marked, (((1,), (1,)), ((), ())), preferred_element_type=f32).astype(bf16)
    row = lax.broadcasted_iota(jnp.int32, (mask.shape[0], ticks), 0)
    column = lax.broadcasted_iota(jnp.int32, (mask.shape[0], ticks), 1)
    return dot(rows, jnp.where(column // BT == row, 1.0, 0.0).astype(bf16))


def chosen_signal(both, inside):
    ticks = inside.shape[1]
    return jnp.where(inside > 0.5, both[:, :ticks], both[:, ticks:])


def scaled_basis(block, blocks, basis, filters, harmonics):
    padded = basis.shape[1] // 2
    ticks = basis.shape[2]
    gains = []
    for gain in filters:
        columns = gain[...] if blocks == 1 else None
        for b in range(blocks):
            piece = gain[:, b * harmonics : (b + 1) * harmonics]
            columns = piece if columns is None else jnp.where(block == b, piece, columns)
        if padded > harmonics:
            columns = jnp.concatenate([columns, jnp.zeros((1, padded - harmonics), f32)], axis=1)
        columns = jnp.concatenate([columns, columns], axis=1)
        tall = jnp.transpose(jnp.broadcast_to(columns, (lane, 2 * padded)))
        gains.append(jnp.concatenate([tall] * (ticks // lane), axis=1))
    values = basis[block]
    return split(jnp.concatenate([values * part for part in gains], axis=1))


def own_signal(blocks, own, basis_source, wide_filter, tight_filter, mask, signal, bases, inside, basis, sem):
    basis_copy = pltpu.make_async_copy(basis_source, basis, sem)
    basis_copy.start()
    inside[...] = spread_mask(mask[...], own.shape[0], signal.shape[1])
    basis_copy.wait()
    here = lax.axis_index("chan")
    ticks = signal.shape[1]
    harmonics = wide_filter.shape[1] // blocks
    filters = (wide_filter, tight_filter)
    high, low = scaled_basis(here, blocks, basis, filters, harmonics)
    joined = jnp.concatenate(split(own[...]), axis=1)
    both = dot(joined, jnp.concatenate([high, high], axis=0))
    both += dot(joined, jnp.concatenate([low, low], axis=0))
    signal[...] = chosen_signal(both, inside[...])
    for shift in range(1, blocks):
        parts = scaled_basis(lax.rem(here + blocks - shift, blocks), blocks, basis, filters, harmonics)
        bases[shift - 1] = jnp.concatenate(parts, axis=0)


def whole_signal(blocks, signal, bases, inside, *refs):
    out = refs[-1]
    both = None
    for shift in range(1, blocks):
        values = refs[shift - 1][...]
        term = dot(jnp.concatenate([values, values], axis=1), bases[shift - 1])
        both = term if both is None else both + term
    if both is None:
        out[...] = signal[...]
    else:
        out[...] = signal[...] + chosen_signal(both, inside[...])


def part_signal(spans, signal, bases, inside, values, *refs):
    out, room, sems = refs[-3:]
    step = room.shape[0] // sems.shape[0]
    for device, (first, count) in enumerate(spans):

        @pl.when(lax.axis_index("chan") == device)
        def _(first=first, count=count):
            copies = []
            for i in range(count // step):
                some = values[i * step : (i + 1) * step, :]
                both = dot(jnp.concatenate([some, some], axis=1), bases[0])
                rows, slot = pl.ds(first + i * step, step), pl.ds(i * step, step)
                room[slot, :] = signal[rows, :] + chosen_signal(both, inside[rows, :])
                copies.append(pltpu.make_async_copy(room.at[slot], out.at[rows], sems.at[i]))
                copies[-1].start()
            for copy in copies:
                copy.wait()


costs = {
    "tick_spectra": 500, "edge_bands": 200, "near_part": 600, "factors": 575, "far_part": 300, "leading_planes": 850, "trailing_planes": 850,
    "own_signal": 500, "part_signal": 250, "all_planes": 2000,
}
costs = {name: cost * 1250000 for name, cost in costs.items()}


def call(kernel, outs, ins, name, scratch=(), final=False, aliases=None):
    kind = jax.ShapeDtypeStruct if final else pltpu.VMEM
    return pl.pallas_call(
        kernel,
        out_shape=[kind(shape, dtype) for shape, dtype in outs],
        in_specs=ins,
        out_specs=[pinned if final else whole] * len(outs),
        scratch_shapes=scratch,
        compiler_params=pltpu.CompilerParams(vmem_limit_bytes=28 * 1024 * 1024),
        cost_estimate=pl.CostEstimate(flops=costs[name], bytes_accessed=0, transcendentals=0),
        input_output_aliases=aliases or {},
        name=name,
    )


def body(frames, link_to_wire, neighbours, kernel, wide_filter, tight_filter, roi_mask):
    frames, roi_mask = frames[0], roi_mask[0]
    share, ticks = frames.shape
    blocks = lax.axis_size("chan")
    detectors = lax.axis_size("apa")
    padded = max(kernel.shape[1], lane // 2)
    width = 2 * padded
    wires = link_to_wire if share % lane == 0 else link_to_wire.reshape(blocks, share)
    table = jnp.asarray(forward_tables(ticks, blocks, padded))

    def around(parts):
        return [
            lax.ppermute(part, "chan", [(i, (i + s) % blocks) for i in range(blocks)])
            for s, part in enumerate(parts, 1)
        ]

    first = call(
        functools.partial(tick_spectra, blocks),
        [((share, width), bf16)] * (blocks - 1)
        + [((share, ticks), bf16), ((blocks, ticks, width), bf16), (wires.shape, jnp.int32), (neighbours.shape, jnp.int32)],
        [pinned] * 4, "tick_spectra", [pltpu.SemaphoreType.DMA((7,))],
    )(*map(distant, (frames, table, wires, neighbours)))
    frames, table, wires, neighbours = map(near, first[blocks - 1 :])
    received = list(map(near, around(first[: blocks - 1])))
    bands = call(
        functools.partial(edge_bands, blocks), [((blocks * HALO_CH, width), bf16)] * 2, [whole] * 4, "edge_bands",
    )(neighbours, frames, table, wires)
    narrow = jnp.asarray(channel_tables(planes[0].length, planes[0].rows, [(i, slice(None)) for i in (0, 1, 0)]))
    wide = jnp.asarray(channel_tables(planes[2].length, planes[2].rows, [(i, part) for part in (inner, edge) for i in (0, 1)]))
    sources = [kernel, wide]
    folded, *ready = call(
        lambda *refs: near_part(refs[: len(sources)], *refs[len(sources) :]),
        [((all_rows, 2 * width), f32)] + [(part.shape, part.dtype) for part in sources],
        [pinned] * len(sources) + [whole] * 3, "near_part", [pltpu.SemaphoreType.DMA((len(sources),))],
    )(*map(distant, sources), wires, frames, table)
    halo = []
    for way, band in enumerate(bands):
        pairs = [(a, partners(a)[way]) for a in range(detectors) if 0 <= partners(a)[way] < detectors]
        halo.append(lax.ppermute(band, "apa", pairs))
    *halo, folded = lax.optimization_barrier((*halo, folded))
    shares = [
        jnp.concatenate([band[s * HALO_CH : (s + 1) * HALO_CH] for band in halo]) for s in range(1, blocks)
    ]
    halo = [near(band) for band in halo + around(shares)]
    kernel, wide = map(near, ready)
    folded = near(folded)
    spare_rows = (blocks - 1) * share
    both = ((all_rows, 2 * width), f32)
    sums, diffs, chosen, far_signs, narrow = map(near, call(
        functools.partial(factors, blocks, share),
        [both, both, ((all_rows, spare_rows), bf16), ((spare_rows, width), f32), (narrow.shape, bf16)],
        [whole] * 2 + [pinned], "factors", [pltpu.SemaphoreType.DMA],
    )(kernel, wires, distant(narrow)))
    single = ((planes[2].rows, width), f32)
    folded, *parts = call(
        functools.partial(far_part, blocks - 1), [both, single, single], [whole] * (blocks + 3), "far_part",
    )(*received, chosen, far_signs, folded, wide)
    operands = (neighbours, *halo, near(folded), sums, diffs, narrow, wide)
    basis = jnp.asarray(inverse_tables(ticks, blocks, padded))
    filters = (wide_filter[None], tight_filter[None])
    mask = jnp.transpose(roi_mask)
    signal_shapes = [
        ((share, ticks), f32), ((max(blocks - 1, 1), 2 * width, 2 * ticks), bf16), ((share, ticks), f32)
    ]

    def own_part(own):
        return call(
            functools.partial(own_signal, blocks), signal_shapes,
            [whole, pinned] + [whole] * 3, "own_signal",
            [pltpu.VMEM(basis.shape, f32), pltpu.SemaphoreType.DMA],
        )(near(own), distant(basis), *filters, mask)

    if blocks != 2:
        own, *sends = call(
            functools.partial(all_planes, blocks, share),
            [((share, width), f32)] + [((share, width), bf16)] * (blocks - 1),
            [whole] * (blocks + 7), "all_planes",
            [pltpu.VMEM((CHANNELS, width), f32)],
        )(*operands)
        returned = map(near, around(sends))
        signal, bases, inside = own_part(own)
        out = pl.pallas_call(
            functools.partial(whole_signal, blocks),
            out_shape=jax.ShapeDtypeStruct((share, ticks), f32),
            in_specs=[whole] * (blocks + 2),
            out_specs=whole,
            name="whole_signal",
        )(*map(near, (signal, bases, inside)), *returned)
        return out[None]

    below, above = share - PU, PU + PV - share
    sent, rest = call(
        leading_planes, [((PU, width), bf16), ((PV, width), f32)],
        [whole] * 11, "leading_planes", [pltpu.VMEM((PU + PV, width), f32)],
    )(*operands, *map(near, parts))
    (early,) = map(near, around([sent]))
    sent, own = call(
        trailing_planes, [((below, width), bf16), ((share, width), f32)],
        [whole] * 10, "trailing_planes", [pltpu.VMEM((PU + PV, width), f32)],
    )(*operands, near(rest))
    signal, bases, inside = own_part(own)
    signal = near(signal)
    (late,) = map(near, around([sent]))

    def finish(values, spans, *before):
        step = values.shape[0] // 2
        rows = max(count for _, count in spans)
        (out,) = call(
            functools.partial(part_signal, spans), [((share, ticks), f32)],
            [whole] * 4 + [pinned] * len(before), "part_signal",
            [pltpu.VMEM((rows, ticks), f32), pltpu.SemaphoreType.DMA((rows // step,))],
            final=True, aliases={4: 0} if before else None,
        )(signal, near(bases), near(inside), values, *before)
        return out

    out = finish(early, ((0, PU), (below, PU)))
    return finish(late, ((PU, below), (0, below)), out)[None]


def solution(mesh):
    placed = (
        P("apa", "chan", None),
        P("apa", None),
        P("apa", None),
        P(None, "chan", None),
        P(),
        P(),
        P("apa", "chan", None),
    )
    return jax.shard_map(
        body, mesh=mesh, in_specs=placed, out_specs=P("apa", "chan", None), check_vma=False
    )
```
